512 devices in a mesh: sec: 2 (over core), wide: 32 (over z, x), narrow: 8 (over y).
Axes of the slice: x: 4, y: 8, z: 8, core: 2. Of those that a mesh axis runs over, the one named last changes fastest.
Arguments:
- voltages: bfloat16 [2, 32, 64, 2, 2, 32768], P('sec', None, 'wide', None, None, 'narrow'), may hold values from -6 to 6
- prototype: float32 [16, 256], replicated, may hold values from -1.5 to 1.5
- beam_delays: float32 [128, 64], replicated, may hold values from -0.5 to 0.5
- station_shifts: int32 [64], P('wide'), may hold values from 0 to 128, as said below
- dm_index: int32 [32], replicated, may hold values from 1 to 63
- owners: int32 [32], replicated, may hold values from 0 to 31, as said below
Outputs:
- power: float32 [2, 64, 128, 128], P('sec', 'wide', 'narrow')
The draws below stay inside these ranges and needn't reach their ends.
Inputs may be any that keep to these rules, and one draw needn't show every extreme that they name: `owners`: no index along wide owns more than 2 subbands, and some index owns exactly 2. `station_shifts`: some station's shift is exactly 128.
All inputs are finite; a program needn't handle non-finite values.
Results may differ from the reference program's by a relative error of at most 0.00069.
Values may be sent and summed in bfloat16 or wider, within the bound.
No kernel may reach another device: no remote copies, remote signals or barrier semaphores. Data moves between devices by JAX's collectives and lax.ppermute only.
A program may use at most 128 MiB of HBM per device.

```python
import math
import jax
import jax.numpy as jnp
from jax import lax

STATIONS = 64
POLS = 2
CH = 256
TAPS = 16
HALF_JOB_BEAMS = 128
MAXD = 128
SEG = 16
SAMPLE_BLOCKS = 2
SB = 32
SUBBAND_LIMIT = 2
LIST_SLOTS = 64
BLOCK_SPECTRA = 128
DL = 32


def draw_station_shifts(key, part):
    first_key, second_key = jax.random.split(key)
    base_shift = jax.random.randint(first_key, (STATIONS,), 0, MAXD + 1)
    chosen = jax.random.randint(second_key, (), 0, STATIONS)
    station_ids = jnp.arange(STATIONS)
    return jnp.where(station_ids == chosen, MAXD, base_shift).astype(jnp.int32)


def draw_owners(key, part):
    complete_key, sorting_key, mix_key = jax.random.split(key, 3)
    complete_owner = jax.random.randint(complete_key, (), 0, LIST_SLOTS // SUBBAND_LIMIT)
    slot_ranking = jax.random.permutation(sorting_key, LIST_SLOTS)
    slot_numbers = jnp.arange(LIST_SLOTS)
    scores = jnp.where(slot_numbers // SUBBAND_LIMIT == complete_owner, slot_numbers % SUBBAND_LIMIT - SUBBAND_LIMIT, slot_ranking)
    chosen = jnp.argsort(scores)[:SB]
    owner_ids = (chosen // SUBBAND_LIMIT)[jax.random.permutation(mix_key, SB)]
    return owner_ids.astype(jnp.int32)


def set_ends(array, rng, least, high):
    extent = array.shape
    place = [jax.random.randint(jax.random.fold_in(rng, axis), (), 0, extent[axis]) for axis in range(len(extent))]
    array = array.at[tuple(place)].set(least)
    longest = extent.index(max(extent))
    place[longest] = (place[longest] + 1) % extent[longest]
    return array.at[tuple(place)].set(high)


def steps_of(rng, extent, cuts, low, high):
    factor_of, own = 1.0, jax.random.fold_in(rng, 6)
    for dim, blocks in cuts:
        heights = jnp.exp(jax.random.uniform(jax.random.fold_in(own, dim), (blocks,), jnp.float32, low / len(cuts), high / len(cuts)))
        factor_of = factor_of * jnp.repeat(heights, extent[dim] // blocks).reshape([-1 if axis == dim else 1 for axis in range(len(extent))])
    return factor_of


def scatter_about(own_key, extent, deviation, reach, cuts=(), kind=jnp.bfloat16):
    drawn = deviation * jax.random.normal(own_key, extent, jnp.float32)
    if cuts:
        drawn = drawn * steps_of(own_key, extent, cuts, -0.22, 0.18)
    return jnp.clip(drawn, -reach, reach).astype(kind)


def setup_inputs(seed: int = 0) -> dict:
    key_list = jax.random.split(jax.random.key(seed), 7)
    return {
        "voltages": scatter_about(key_list[0], (SAMPLE_BLOCKS, SB, STATIONS, POLS, 2, BLOCK_SPECTRA * CH), 1.0, 6.0, ((0, 2), (2, 32), (5, 8))),
        "prototype": scatter_about(key_list[1], (TAPS, CH), TAPS ** -0.5, 1.5, (), jnp.float32),
        "beam_delays": jnp.clip(jax.random.uniform(key_list[2], (HALF_JOB_BEAMS, STATIONS), jnp.float32, -0.5, 0.5), -0.5, 0.5),
        "station_shifts": draw_station_shifts(jax.random.fold_in(key_list[6], 71), 0),
        "dm_index": set_ends(jax.random.randint(key_list[4], (SB,), 1, 2 * DL), jax.random.fold_in(key_list[4], 1), 1, (2 * DL) - 1).astype(jnp.int32),
        "owners": draw_owners(jax.random.fold_in(key_list[6], 71), 0),
    }


TWO_PI = 2.0 * math.pi

def beamset_slot_tables(owners, slot_count, capacity):
    sub_count = owners.shape[0]
    sub_order = jnp.arange(sub_count, dtype=jnp.int32)
    same_owner = owners[:, None] == owners[None, :]
    before = sub_order[None, :] < sub_order[:, None]
    rank_in_set = lax.optimization_barrier(jnp.sum(jnp.where(same_owner & before, 1, 0), axis=1)).astype(jnp.int32)
    slot_lookup = (owners * capacity + rank_in_set).astype(jnp.int32)
    slot_numbers = jnp.arange(slot_count, dtype=jnp.int32)
    slot_match = slot_lookup[None, :] == slot_numbers[:, None]
    subband_per_slot = lax.optimization_barrier(jnp.sum(jnp.where(slot_match, sub_order[None, :], 0), axis=1)).astype(jnp.int32)
    filled_slots = jnp.any(slot_match, axis=1)
    return (slot_lookup, subband_per_slot, filled_slots)

def beam_weights(subs, channels, chan_count, beam_delays):
    frequency = subs.astype(jnp.float32)[:, None] + channels.astype(jnp.float32)[None, :] / chan_count
    phase_arg = (TWO_PI * frequency)[:, :, None, None] * beam_delays[None, None, :, :]
    norm_scale = 1.0 / math.sqrt(beam_delays.shape[1])
    weight_real = (jnp.cos(phase_arg) * norm_scale).astype(jnp.bfloat16)
    weight_imag = (-jnp.sin(phase_arg) * norm_scale).astype(jnp.bfloat16)
    upper = jnp.stack([weight_real, -weight_imag], axis=4)
    lower = jnp.stack([weight_imag, weight_real], axis=4)
    return jnp.stack([upper, lower], axis=3)

def chirp_matrix(dm_values, channels, seg_len):
    dft_len = 2 * seg_len
    bin_index = jnp.arange(dft_len, dtype=jnp.int32)
    signed = jnp.where(bin_index < dft_len // 2, bin_index, bin_index - dft_len)
    phase_index = jnp.mod(dm_values[:, None, None] * signed[None, None, :] * (signed[None, None, :] + channels[None, :, None]), 2 * dft_len)
    offsets = jnp.arange(dft_len, dtype=jnp.int32)
    angle_index = jnp.mod(phase_index[:, :, None, :] + 2 * offsets[None, None, :, None] * bin_index[None, None, None, :], 2 * dft_len)
    angles = angle_index.astype(jnp.float32) * (math.pi / dft_len)
    kern_real = lax.optimization_barrier(jnp.sum(jnp.cos(angles), axis=-1)) / dft_len
    kern_imag = lax.optimization_barrier(jnp.sum(jnp.sin(angles), axis=-1)) / dft_len
    row_ids = jnp.arange(seg_len, dtype=jnp.int32)
    lag_index = jnp.mod(row_ids[:, None] + seg_len - offsets[None, :], dft_len)
    mat_real = jnp.take(kern_real, lag_index, axis=-1).astype(jnp.bfloat16)
    mat_imag = jnp.take(kern_imag, lag_index, axis=-1).astype(jnp.bfloat16)
    upper = jnp.stack([mat_real, -mat_imag], axis=3)
    lower = jnp.stack([mat_imag, mat_real], axis=3)
    return jnp.stack([upper, lower], axis=2)

def reference(voltages, prototype, beam_delays, station_shifts, dm_index, owners):
    slot_lookup, subband_per_slot, filled_slots = beamset_slot_tables(owners, LIST_SLOTS, SUBBAND_LIMIT)
    chan_ids = jnp.arange(CH, dtype=jnp.int32)
    span_len = (BLOCK_SPECTRA + TAPS - 1) * CH

    def delay_one(samples, offset):
        return lax.dynamic_slice_in_dim(samples, offset, span_len, axis=-1)

    def one_subband(sub_idx):
        sub_volts = lax.dynamic_index_in_dim(voltages, sub_idx, axis=1, keepdims=False)
        weights = beam_weights(sub_idx[None], chan_ids, CH, beam_delays)[0]
        chirp_mat = chirp_matrix(lax.dynamic_index_in_dim(dm_index, sub_idx, axis=0, keepdims=True), chan_ids, SEG)[0]
        earlier = jnp.zeros((CH, HALF_JOB_BEAMS, 2, POLS, SEG), jnp.bfloat16)
        powers = []
        for block_idx in range(SAMPLE_BLOCKS):
            block_volts = sub_volts[block_idx]
            padding = jnp.zeros(block_volts.shape[:-1] + ((TAPS - 1) * CH + MAXD,), jnp.bfloat16)
            extended = jnp.concatenate([block_volts, padding], axis=-1)
            shifted = jax.vmap(delay_one)(extended, station_shifts)
            frames = shifted.reshape(STATIONS, POLS, 2, BLOCK_SPECTRA + TAPS - 1, CH)
            filtered = jnp.zeros((STATIONS, POLS, 2, BLOCK_SPECTRA, CH), jnp.float32)
            for tap_index in range(TAPS):
                filtered = filtered + frames[:, :, :, tap_index:tap_index + BLOCK_SPECTRA, :].astype(jnp.float32) * prototype[tap_index]
            spectrum = jnp.fft.fft(lax.complex(filtered[:, :, 0], filtered[:, :, 1]), axis=-1) / math.sqrt(CH)
            stacked = jnp.stack([jnp.real(spectrum), jnp.imag(spectrum)], axis=2).astype(jnp.bfloat16)
            beam_data = jnp.einsum('cbysx,spxtc->cbypt', weights.astype(jnp.float32), stacked.astype(jnp.float32)).astype(jnp.bfloat16)
            series = jnp.concatenate([earlier, beam_data], axis=-1)
            early_half = series[..., :BLOCK_SPECTRA].reshape(CH, HALF_JOB_BEAMS, 2, POLS, BLOCK_SPECTRA // SEG, SEG)
            late_half = series[..., SEG:].reshape(CH, HALF_JOB_BEAMS, 2, POLS, BLOCK_SPECTRA // SEG, SEG)
            cleaned = jnp.einsum('cyjxe,cbxpge->cbypgj', chirp_mat[..., :SEG].astype(jnp.float32), early_half.astype(jnp.float32))
            cleaned = cleaned + jnp.einsum('cyjxe,cbxpge->cbypgj', chirp_mat[..., SEG:].astype(jnp.float32), late_half.astype(jnp.float32))
            powers.append((lax.optimization_barrier(jnp.sum(cleaned * cleaned, axis=(0, 2, 3))) / CH).reshape(HALF_JOB_BEAMS, BLOCK_SPECTRA))
            earlier = beam_data[..., BLOCK_SPECTRA - SEG:]
        return jnp.stack(powers, axis=0)
    per_sub = lax.map(one_subband, jnp.arange(SB, dtype=jnp.int32))
    final_result = jnp.zeros((SAMPLE_BLOCKS, LIST_SLOTS, HALF_JOB_BEAMS, BLOCK_SPECTRA), jnp.float32)
    return final_result.at[:, slot_lookup].set(jnp.transpose(per_sub, (1, 0, 2, 3)))
```

```python
import math

import jax
import jax.numpy as jnp
from jax import lax
from jax.experimental import pallas as pl
from jax.experimental.pallas import tpu as pltpu
from jax.sharding import PartitionSpec as P

SEG = 16
SUBBAND_LIMIT = 2
TWO_PI = 2.0 * math.pi
VMEM_BYTES = 56 * 1024 * 1024
T_BLOCK = 8


def slot_tables(owners, slot_count):
    sub_count = owners.shape[0]
    order = jnp.arange(sub_count, dtype=jnp.int32)
    same = owners[:, None] == owners[None, :]
    before = order[None, :] < order[:, None]
    rank = jnp.sum(jnp.where(same & before, 1, 0), axis=1).astype(jnp.int32)
    lookup = owners * SUBBAND_LIMIT + rank
    slots = jnp.arange(slot_count, dtype=jnp.int32)
    match = lookup[None, :] == slots[:, None]
    subband = jnp.sum(jnp.where(match, order[None, :], 0), axis=1)
    return subband, jnp.any(match, axis=1)


def filter_kernel(volts_ref, taps_ref, table_ref, out_ref, frames, filtered, packed):
    source_count, group_size, rows, piece_len = volts_ref.shape
    tap_count, _, chan_count = taps_ref.shape
    block_count = 2
    pieces = source_count // block_count
    piece_frames = piece_len // chan_count
    frame_count = pieces * piece_frames
    station_count = table_ref.shape[0]
    pol_count = rows // (2 * station_count)
    frames[frame_count:] = jnp.zeros_like(frames[frame_count:])

    def one(index, carry):
        sub = index // block_count
        block = index % block_count
        for piece in range(pieces):
            for frame in range(piece_frames):
                frames[piece * piece_frames + frame] = volts_ref[
                    block * pieces + piece, sub, :, frame * chan_count : (frame + 1) * chan_count
                ].astype(jnp.float32)
        for low in range(0, chan_count, 128):
            lanes = slice(low, low + 128)
            taps = [taps_ref[tap, :, lanes] for tap in range(tap_count)]

            def some(step, inner):
                start = pl.multiple_of(step * T_BLOCK, T_BLOCK)
                loaded = [frames[start + i, :, lanes] for i in range(T_BLOCK + tap_count - 1)]
                for i in range(T_BLOCK):
                    total = taps[0] * loaded[i]
                    for tap in range(1, tap_count):
                        total = total + taps[tap] * loaded[i + tap]
                    at = pl.multiple_of((start + i) * rows, rows)
                    filtered[low // 128, pl.ds(at, rows), :] = total
                return inner

            lax.fori_loop(0, frame_count // T_BLOCK, some, 0)
        for station in range(station_count):
            parts = []
            for pol in range(pol_count):
                pair = [
                    filtered[
                        half,
                        pl.ds((station * pol_count + pol) * 2 + r, frame_count, stride=rows),
                        :,
                    ].astype(jnp.bfloat16)
                    for r in range(2)
                    for half in range(chan_count // 128)
                ]
                parts.append(jnp.concatenate(pair, axis=1))
            series = jnp.concatenate(parts, axis=0)
            spectra = lax.dot_general(
                table_ref[station],
                series,
                (((1,), (1,)), ((), ())),
                preferred_element_type=jnp.float32,
            )
            for r in range(2):
                for pol in range(pol_count):
                    packed[
                        block, pl.ds((station * 2 + r) * pol_count + pol, chan_count, stride=rows), :
                    ] = spectra[
                        r * chan_count : (r + 1) * chan_count,
                        pol * frame_count : (pol + 1) * frame_count,
                    ]

        @pl.when(block == block_count - 1)
        def _():
            for b in range(block_count):
                out_ref[sub, :, :, b * frame_count : (b + 1) * frame_count] = (
                    packed[b].reshape(chan_count, rows, frame_count).astype(jnp.bfloat16)
                )

        return carry

    lax.fori_loop(0, group_size * block_count, one, 0)


def beam_kernel(spectra_ref, weights_ref, kern_ref, power_ref, held):
    source_count, chan_local, rows, length = spectra_ref.shape
    block_count, beam_count, block_len = power_ref.shape
    pol_count = 2
    depth = source_count * rows // pol_count
    span = 2 * SEG
    from_seg = lax.broadcasted_iota(jnp.int32, (block_len, block_len), 0) // SEG
    to_seg = lax.broadcasted_iota(jnp.int32, (block_len, block_len), 1) // SEG
    own_mask = (from_seg == to_seg) | (from_seg + 1 == to_seg)
    cross_mask = (from_seg == block_len // SEG - 1) & (to_seg == 0)
    power_ref[...] = jnp.zeros_like(power_ref)

    def one(chan, carry):
        for block in range(block_count):
            lanes = slice(block * block_len, (block + 1) * block_len)
            held[block] = (
                spectra_ref[:, chan, :, lanes]
                .astype(jnp.float32)
                .reshape(source_count * rows, block_len)
            )
        inputs = jnp.concatenate(
            [
                held[block, pl.ds(pol, depth, stride=pol_count), :].astype(jnp.bfloat16)
                for pol in range(pol_count)
                for block in range(block_count)
            ],
            axis=1,
        )
        beams = jnp.dot(
            weights_ref[chan], inputs, preferred_element_type=jnp.float32
        ).astype(jnp.bfloat16)
        tiled = [
            jnp.concatenate([kern_ref[chan, part]] * (block_len // span), axis=0)
            for part in range(2)
        ]

        def matrix(mask):
            real, imag = [jnp.where(mask, part, 0.0) for part in tiled]
            return jnp.concatenate(
                [
                    jnp.concatenate([real, imag], axis=1),
                    jnp.concatenate([-imag, real], axis=1),
                ],
                axis=0,
            ).astype(jnp.bfloat16)

        def series(block):
            parts = []
            for pol in range(pol_count):
                at = pol * length + block * block_len
                parts.append(
                    jnp.concatenate(
                        [
                            beams[:beam_count, at : at + block_len],
                            beams[beam_count:, at : at + block_len],
                        ],
                        axis=1,
                    )
                )
            return jnp.concatenate(parts, axis=0)

        own = matrix(own_mask)
        first, second = series(0), series(1)
        clean = [
            jnp.dot(first, own, preferred_element_type=jnp.float32),
            jnp.dot(second, own, preferred_element_type=jnp.float32)
            + jnp.dot(first, matrix(cross_mask), preferred_element_type=jnp.float32),
        ]
        for block in range(block_count):
            square = clean[block] * clean[block]
            both = square[:beam_count] + square[beam_count:]
            power_ref[block] += both[:, :block_len] + both[:, block_len:]
        return carry

    lax.fori_loop(0, chan_local, one, 0)


def shards(voltages, prototype, beam_delays, station_shifts, dm_index, owners):
    wide_count = lax.axis_size("wide")
    source_count = lax.axis_size("sec") * lax.axis_size("narrow")
    narrow_count = lax.axis_size("narrow")
    block_count = lax.axis_size("sec")
    _, sub_count, station_local, pol_count, _, piece_len = voltages.shape
    tap_count, chan_count = prototype.shape
    beam_count, station_count = beam_delays.shape
    rows = station_local * pol_count * 2
    group_size = sub_count // source_count
    chan_local = group_size * chan_count // wide_count
    chan_groups = chan_count // chan_local
    block_len = piece_len * narrow_count // chan_count
    length = block_count * block_len
    together = ("sec", "narrow")

    volts = voltages.reshape(sub_count, rows, piece_len)
    volts = lax.all_to_all(volts, together, 0, 0, tiled=True)
    volts = volts.reshape(source_count, group_size, rows, piece_len)

    flat = prototype.reshape(-1)
    taps = jnp.stack(
        [
            lax.dynamic_update_slice(
                jnp.zeros((tap_count + 1) * chan_count, jnp.float32), flat, (station_shifts[s],)
            ).reshape(tap_count + 1, chan_count)
            for s in range(station_local)
        ],
        axis=1,
    )
    taps = jnp.repeat(taps, 2 * pol_count, axis=1)
    ids = jnp.arange(chan_count, dtype=jnp.int32)
    turn = jnp.mod(
        ids[None, :, None] * (ids[None, None, :] - station_shifts[:, None, None]), chan_count
    )
    angle = turn.astype(jnp.float32) * (TWO_PI / chan_count)
    scale = 1.0 / math.sqrt(chan_count)
    cosine, sine = jnp.cos(angle) * scale, jnp.sin(angle) * scale
    table = jnp.concatenate(
        [
            jnp.concatenate([cosine, sine], axis=2),
            jnp.concatenate([-sine, cosine], axis=2),
        ],
        axis=1,
    ).astype(jnp.bfloat16)
    whole = pl.BlockSpec(memory_space=pltpu.VMEM)
    spectra = pl.pallas_call(
        filter_kernel,
        out_shape=jax.ShapeDtypeStruct((group_size, chan_count, rows, length), jnp.bfloat16),
        in_specs=[whole] * 3,
        out_specs=whole,
        scratch_shapes=[
            pltpu.VMEM((block_len + tap_count, rows, chan_count), jnp.float32),
            pltpu.VMEM((chan_count // 128, block_len * rows, 128), jnp.float32),
            pltpu.VMEM((block_count, chan_count * rows, block_len), jnp.float32),
        ],
        compiler_params=pltpu.CompilerParams(vmem_limit_bytes=VMEM_BYTES),
        name="filter",
    )(volts, taps, table)

    spectra = spectra.reshape(wide_count, chan_local, rows, length)
    spectra = lax.all_to_all(spectra, "wide", 0, 0, tiled=True)

    wide_index = lax.axis_index("wide")
    group = lax.axis_index("sec") * narrow_count + lax.axis_index("narrow")
    member = wide_index // chan_groups
    sub = group * group_size + member
    channels = (wide_index % chan_groups) * chan_local + jnp.arange(chan_local, dtype=jnp.int32)

    frequency = sub.astype(jnp.float32) + channels.astype(jnp.float32) / chan_count
    delays = jnp.repeat(beam_delays, 2, axis=1)
    phase = (TWO_PI * frequency)[:, None, None] * delays[None]
    norm = 1.0 / math.sqrt(station_count)
    cosine, sine = jnp.cos(phase) * norm, jnp.sin(phase) * norm
    is_real = jnp.arange(2 * station_count)[None, None, :] % 2 == 0
    weights = jnp.concatenate(
        [jnp.where(is_real, cosine, sine), jnp.where(is_real, -sine, cosine)], axis=1
    ).astype(jnp.bfloat16)

    span = 2 * SEG
    bins = jnp.arange(span, dtype=jnp.int32)
    signed = jnp.where(bins < span // 2, bins, bins - span)
    dm_value = jnp.sum(jnp.where(jnp.arange(sub_count) == sub, dm_index, 0))
    phase_index = dm_value * signed[None, :] * (signed[None, :] + channels[:, None])
    angle_index = jnp.mod(
        phase_index[:, None, :] + 2 * bins[None, :, None] * bins[None, None, :], 2 * span
    )
    angles = angle_index.astype(jnp.float32) * (math.pi / span)
    kern = jnp.stack(
        [jnp.sum(jnp.cos(angles), axis=-1) / span, jnp.sum(jnp.sin(angles), axis=-1) / span],
        axis=1,
    ).astype(jnp.bfloat16)
    lag = jnp.mod(jnp.arange(block_len)[None, :] - bins[:, None], span)
    pick = (lag[None] == bins[:, None, None]).astype(jnp.bfloat16)
    kern = jnp.einsum("crd,dab->crab", kern, pick, preferred_element_type=jnp.float32)

    partial = pl.pallas_call(
        beam_kernel,
        out_shape=jax.ShapeDtypeStruct((block_count, beam_count, block_len), jnp.float32),
        in_specs=[whole] * 3,
        out_specs=whole,
        scratch_shapes=[pltpu.VMEM((block_count, wide_count * rows, block_len), jnp.float32)],
        compiler_params=pltpu.CompilerParams(vmem_limit_bytes=VMEM_BYTES),
        name="beams",
    )(spectra, weights, kern)

    partial = partial.reshape(source_count, beam_count // narrow_count, block_len)
    partial = lax.all_to_all(partial, together, 0, 0, tiled=True)
    slot_count = wide_count * SUBBAND_LIMIT
    slot_sub, filled = slot_tables(owners, slot_count)
    mine = filled & (slot_sub % group_size == member)
    outgoing = jnp.where(
        mine[:, None, None], jnp.take(partial, slot_sub // group_size, axis=0), 0.0
    )
    arrived = lax.all_to_all(outgoing, "wide", 0, 0, tiled=True)
    arrived = arrived.reshape(wide_count, SUBBAND_LIMIT, beam_count // narrow_count, block_len)
    return (jnp.sum(arrived, axis=0) / chan_count)[None]


def solution(mesh):
    placed = (P("sec", None, "wide", None, None, "narrow"), P(), P(), P("wide"), P(), P())
    return jax.shard_map(
        shards,
        mesh=mesh,
        in_specs=placed,
        out_specs=P("sec", "wide", "narrow", None),
        check_vma=False,
    )
```

```python
import math

import jax
import jax.numpy as jnp
from jax import lax
from jax.experimental import pallas as pl
from jax.experimental.pallas import tpu as pltpu
from jax.sharding import PartitionSpec as P

SEG = 16
SUBBAND_LIMIT = 2
TWO_PI = 2.0 * math.pi
VMEM_BYTES = 56 * 1024 * 1024
T_BLOCK = 8


def slot_tables(owners, slot_count):
    sub_count = owners.shape[0]
    order = jnp.arange(sub_count, dtype=jnp.int32)
    same = owners[:, None] == owners[None, :]
    before = order[None, :] < order[:, None]
    rank = jnp.sum(jnp.where(same & before, 1, 0), axis=1).astype(jnp.int32)
    lookup = owners * SUBBAND_LIMIT + rank
    slots = jnp.arange(slot_count, dtype=jnp.int32)
    match = lookup[None, :] == slots[:, None]
    subband = jnp.sum(jnp.where(match, order[None, :], 0), axis=1)
    return subband, jnp.any(match, axis=1)


def filter_body(place, sources, taps_ref, table_ref, out_ref, frames, filtered, packed):
    tap_count, rows, chan_count = taps_ref.shape
    block_count, row_count, _ = packed.shape
    piece_frames = sources[0].shape[-1] // chan_count
    frame_count = filtered.shape[2] // rows
    station_count = table_ref.shape[0]
    member_count = rows // (2 * station_count)
    halves = chan_count // 128
    quad = 2 * station_count
    frames[frame_count:] = jnp.zeros_like(frames[frame_count:])

    def one(block, carry):
        for number, source in enumerate(sources):
            at, start = place(number, block)
            for frame in range(piece_frames):
                frames[start + frame] = source[
                    at, :, frame * chan_count : (frame + 1) * chan_count
                ].astype(jnp.float32)
        for half in range(halves):
            lanes = slice(half * 128, half * 128 + 128)
            taps = [taps_ref[tap, :, lanes] for tap in range(tap_count)]

            def some(step, inner):
                start = pl.multiple_of(step * T_BLOCK, T_BLOCK)
                loaded = [frames[start + i, :, lanes] for i in range(T_BLOCK + tap_count - 1)]
                for i in range(T_BLOCK):
                    total = taps[0] * loaded[i]
                    for tap in range(1, tap_count):
                        total = total + taps[tap] * loaded[i + tap]
                    at = pl.multiple_of((start + i) * rows, rows)
                    filtered[block, half, pl.ds(at, rows), :] = total
                return inner

            lax.fori_loop(0, frame_count // T_BLOCK, some, 0)
        return carry

    lax.fori_loop(0, block_count, one, 0)

    for member in range(member_count):
        for station in range(station_count):
            parts = []
            for block in range(block_count):
                pair = [
                    filtered[
                        block,
                        half,
                        pl.ds((member * station_count + station) * 2 + r, frame_count, stride=rows),
                        :,
                    ].astype(jnp.bfloat16)
                    for r in range(2)
                    for half in range(halves)
                ]
                parts.append(jnp.concatenate(pair, axis=1))
            spectra = lax.dot_general(
                table_ref[station],
                jnp.concatenate(parts, axis=0),
                (((1,), (1,)), ((), ())),
                preferred_element_type=jnp.float32,
            )
            for r in range(2):
                for block in range(block_count):
                    packed[block, pl.ds(station * 2 + r, chan_count, stride=quad), :] = spectra[
                        r * chan_count : (r + 1) * chan_count,
                        block * frame_count : (block + 1) * frame_count,
                    ]
        for block in range(block_count):
            out_ref[member, :, block * frame_count : (block + 1) * frame_count] = packed[
                block
            ].astype(jnp.bfloat16)


def filter_first(volts_ref, after_ref, *refs):
    taps_ref, packed = refs[0], refs[-1]
    pieces = volts_ref.shape[0] // packed.shape[0]
    step = volts_ref.shape[-1] // taps_ref.shape[-1]

    def place(piece, block):
        return block * pieces + piece, piece * step

    filter_body(place, [volts_ref] * pieces, *refs)


def filter_second(where_ref, *refs):
    pieces = len(refs) - 6
    sources, refs = refs[:pieces], refs[pieces:]
    step = sources[0].shape[-1] // refs[0].shape[-1]

    def place(distance, block):
        piece = lax.rem(where_ref[1] + (pieces - distance), pieces)
        return lax.rem(block + where_ref[0], 2), piece * step

    filter_body(place, sources, *refs)


def turn_kernel(where_ref, pair_ref, after_ref, *refs):
    outs, sems = refs[:-1], refs[-1]
    pieces = len(outs)
    copies = []
    for distance, out in enumerate(outs):
        piece = lax.rem(where_ref[1] + distance, pieces)
        copies.append(pltpu.make_async_copy(pair_ref.at[:, piece], out, sems.at[distance]))
    for copy in copies:
        copy.start()
    for copy in copies:
        copy.wait()


def beam_body(spectra_ref, weights_ref, kern_ref, power_ref, held):
    source_count, row_count, length = spectra_ref.shape
    block_count, beam_count, block_len = power_ref.shape
    chan_local = weights_ref.shape[0]
    quad = row_count // chan_local
    step_chans = held.shape[1] // (source_count * quad)
    step_rows = step_chans * quad
    span = 2 * SEG
    from_seg = lax.broadcasted_iota(jnp.int32, (block_len, block_len), 0) // SEG
    to_seg = lax.broadcasted_iota(jnp.int32, (block_len, block_len), 1) // SEG
    own_mask = (from_seg == to_seg) | (from_seg + 1 == to_seg)
    cross_mask = (from_seg == block_len // SEG - 1) & (to_seg == 0)

    def one(step, carry):
        at = pl.multiple_of(step * step_rows, step_rows)
        for block in range(block_count):
            held[block] = (
                spectra_ref[:, pl.ds(at, step_rows), block * block_len : (block + 1) * block_len]
                .astype(jnp.float32)
                .reshape(source_count * step_rows, block_len)
            )
        for inner in range(step_chans):
            chan = step * step_chans + inner
            inputs = jnp.concatenate(
                [
                    jnp.concatenate(
                        [
                            held[
                                block, pl.ds(inner * quad + q, source_count, stride=step_rows), :
                            ].astype(jnp.bfloat16)
                            for q in range(quad)
                        ],
                        axis=0,
                    )
                    for block in range(block_count)
                ],
                axis=1,
            )
            beams = jnp.dot(
                weights_ref[chan], inputs, preferred_element_type=jnp.float32
            ).astype(jnp.bfloat16)
            tiled = [
                jnp.concatenate([kern_ref[chan, part]] * (block_len // span), axis=0)
                for part in range(2)
            ]

            def matrix(mask):
                real, imag = [jnp.where(mask, part, 0.0) for part in tiled]
                return jnp.concatenate(
                    [
                        jnp.concatenate([real, imag], axis=1),
                        jnp.concatenate([-imag, real], axis=1),
                    ],
                    axis=0,
                ).astype(jnp.bfloat16)

            series = [
                jnp.concatenate(
                    [
                        beams[part * beam_count : (part + 1) * beam_count, low : low + block_len]
                        for part in range(2)
                    ],
                    axis=1,
                )
                for low in range(0, length, block_len)
            ]
            own = jnp.dot(
                jnp.concatenate(series, axis=0),
                matrix(own_mask),
                preferred_element_type=jnp.float32,
            )
            cross = jnp.dot(series[0], matrix(cross_mask), preferred_element_type=jnp.float32)
            clean = [own[:beam_count], own[beam_count:] + cross]
            for block in range(block_count):
                square = clean[block] * clean[block]
                power_ref[block] += square[:, :block_len] + square[:, block_len:]
        return carry

    lax.fori_loop(0, chan_local // step_chans, one, 0)


def beam_first(spectra_ref, weights_ref, kern_ref, power_ref, held):
    power_ref[...] = jnp.zeros_like(power_ref)
    beam_body(spectra_ref, weights_ref, kern_ref, power_ref, held)


def beam_second(spectra_ref, weights_ref, kern_ref, before_ref, power_ref, held):
    power_ref[...] = before_ref[...]
    beam_body(spectra_ref, weights_ref, kern_ref, power_ref, held)


def shards(voltages, prototype, beam_delays, station_shifts, dm_index, owners):
    wide_count = lax.axis_size("wide")
    source_count = lax.axis_size("sec") * lax.axis_size("narrow")
    narrow_count = lax.axis_size("narrow")
    block_count = lax.axis_size("sec")
    _, sub_count, station_local, pol_count, _, piece_len = voltages.shape
    tap_count, chan_count = prototype.shape
    beam_count, station_count = beam_delays.shape
    group_size = sub_count // source_count
    rows = group_size * station_local * 2
    quad = station_local * 2
    chan_local = group_size * chan_count // wide_count
    chan_groups = chan_count // chan_local
    block_len = piece_len * narrow_count // chan_count
    length = block_count * block_len
    together = ("sec", "narrow")
    whole = pl.BlockSpec(memory_space=pltpu.VMEM)
    anywhere = pl.BlockSpec(memory_space=pl.ANY)
    scalars = pl.BlockSpec(memory_space=pltpu.SMEM)
    params = pltpu.CompilerParams(vmem_limit_bytes=VMEM_BYTES)
    where = jnp.stack([lax.axis_index("sec"), lax.axis_index("narrow")]).astype(jnp.int32)

    first, second = [
        voltages[0, :, :, pol].reshape(source_count, rows, piece_len) for pol in range(pol_count)
    ]
    first = lax.all_to_all(first, together, 0, 0, tiled=True)

    second = second.reshape(block_count, narrow_count, rows, piece_len)
    mine = lax.dynamic_index_in_dim(second, where[0], 0, keepdims=False)
    theirs = lax.dynamic_index_in_dim(second, 1 - where[0], 0, keepdims=False)
    pair = jnp.stack([mine, lax.ppermute(theirs, "sec", [(0, 1), (1, 0)])])
    turned = pl.pallas_call(
        turn_kernel,
        out_shape=[
            jax.ShapeDtypeStruct((block_count, rows, piece_len), jnp.bfloat16)
        ] * narrow_count,
        in_specs=[scalars, anywhere, anywhere],
        out_specs=[anywhere] * narrow_count,
        scratch_shapes=[pltpu.SemaphoreType.DMA((narrow_count,))],
        name="turn",
    )(where, pair, first)
    moved = [turned[0]] + [
        lax.ppermute(
            turned[distance],
            "narrow",
            [(i, (i + distance) % narrow_count) for i in range(narrow_count)],
        )
        for distance in range(1, narrow_count)
    ]

    flat = prototype.reshape(-1)
    taps = jnp.stack(
        [
            lax.dynamic_update_slice(
                jnp.zeros((tap_count + 1) * chan_count, jnp.float32), flat, (station_shifts[s],)
            ).reshape(tap_count + 1, chan_count)
            for s in range(station_local)
        ],
        axis=1,
    )
    taps = jnp.tile(jnp.repeat(taps, 2, axis=1), (1, group_size, 1))
    ids = jnp.arange(chan_count, dtype=jnp.int32)
    turn = jnp.mod(
        ids[None, :, None] * (ids[None, None, :] - station_shifts[:, None, None]), chan_count
    )
    angle = turn.astype(jnp.float32) * (TWO_PI / chan_count)
    scale = 1.0 / math.sqrt(chan_count)
    cosine, sine = jnp.cos(angle) * scale, jnp.sin(angle) * scale
    table = jnp.concatenate(
        [
            jnp.concatenate([cosine, sine], axis=2),
            jnp.concatenate([-sine, cosine], axis=2),
        ],
        axis=1,
    ).astype(jnp.bfloat16)
    filter_args = dict(
        out_shape=jax.ShapeDtypeStruct((group_size, chan_count * quad, length), jnp.bfloat16),
        out_specs=whole,
        scratch_shapes=[
            pltpu.VMEM((block_len + tap_count, rows, chan_count), jnp.float32),
            pltpu.VMEM((block_count, chan_count // 128, block_len * rows, 128), jnp.float32),
            pltpu.VMEM((block_count, chan_count * quad, block_len), jnp.float32),
        ],
        compiler_params=params,
    )

    def to_stations(spectra):
        spectra = spectra.reshape(wide_count, chan_local * quad, length)
        return lax.all_to_all(spectra, "wide", 0, 0, tiled=True)

    spectra_first = to_stations(
        pl.pallas_call(
            filter_first,
            in_specs=[whole, anywhere, whole, whole],
            name="filter0",
            **filter_args,
        )(first, turned[0], taps, table)
    )
    spectra_second = to_stations(
        pl.pallas_call(
            filter_second,
            in_specs=[scalars] + [whole] * (narrow_count + 2),
            name="filter1",
            **filter_args,
        )(where, *moved, taps, table)
    )

    wide_index = lax.axis_index("wide")
    group = lax.axis_index("sec") * narrow_count + lax.axis_index("narrow")
    member = wide_index // chan_groups
    sub = group * group_size + member
    channels = (wide_index % chan_groups) * chan_local + jnp.arange(chan_local, dtype=jnp.int32)

    frequency = sub.astype(jnp.float32) + channels.astype(jnp.float32) / chan_count
    delays = jnp.transpose(beam_delays.reshape(beam_count, wide_count, station_local), (0, 2, 1))
    delays = jnp.repeat(delays, 2, axis=1).reshape(beam_count, 2 * station_count)
    phase = (TWO_PI * frequency)[:, None, None] * delays[None]
    norm = 1.0 / math.sqrt(station_count)
    cosine, sine = jnp.cos(phase) * norm, jnp.sin(phase) * norm
    is_real = jnp.arange(2 * station_count)[None, None, :] // wide_count % 2 == 0
    weights = jnp.concatenate(
        [jnp.where(is_real, cosine, sine), jnp.where(is_real, -sine, cosine)], axis=1
    ).astype(jnp.bfloat16)

    span = 2 * SEG
    bins = jnp.arange(span, dtype=jnp.int32)
    signed = jnp.where(bins < span // 2, bins, bins - span)
    dm_value = jnp.sum(jnp.where(jnp.arange(sub_count) == sub, dm_index, 0))
    phase_index = dm_value * signed[None, :] * (signed[None, :] + channels[:, None])
    angle_index = jnp.mod(
        phase_index[:, None, :] + 2 * bins[None, :, None] * bins[None, None, :], 2 * span
    )
    angles = angle_index.astype(jnp.float32) * (math.pi / span)
    kern = jnp.stack(
        [jnp.sum(jnp.cos(angles), axis=-1) / span, jnp.sum(jnp.sin(angles), axis=-1) / span],
        axis=1,
    ).astype(jnp.bfloat16)
    lag = jnp.mod(jnp.arange(block_len)[None, :] - bins[:, None], span)
    pick = (lag[None] == bins[:, None, None]).astype(jnp.bfloat16)
    kern = jnp.einsum("crd,dab->crab", kern, pick, preferred_element_type=jnp.float32)

    beam_args = dict(
        out_shape=jax.ShapeDtypeStruct((block_count, beam_count, block_len), jnp.float32),
        out_specs=whole,
        scratch_shapes=[pltpu.VMEM((block_count, wide_count * 8, block_len), jnp.float32)],
        compiler_params=params,
    )
    partial = pl.pallas_call(beam_first, in_specs=[whole] * 3, name="beams0", **beam_args)(
        spectra_first, weights, kern
    )
    partial = pl.pallas_call(beam_second, in_specs=[whole] * 4, name="beams1", **beam_args)(
        spectra_second, weights, kern, partial
    )

    partial = partial.reshape(source_count, beam_count // narrow_count, block_len)
    partial = lax.all_to_all(partial, together, 0, 0, tiled=True)
    slot_count = wide_count * SUBBAND_LIMIT
    slot_sub, filled = slot_tables(owners, slot_count)
    mine = filled & (slot_sub % group_size == member)
    outgoing = jnp.where(
        mine[:, None, None], jnp.take(partial, slot_sub // group_size, axis=0), 0.0
    )
    arrived = lax.all_to_all(outgoing, "wide", 0, 0, tiled=True)
    arrived = arrived.reshape(wide_count, SUBBAND_LIMIT, beam_count // narrow_count, block_len)
    return (jnp.sum(arrived, axis=0) / chan_count)[None]


def solution(mesh):
    placed = (P("sec", None, "wide", None, None, "narrow"), P(), P(), P("wide"), P(), P())
    return jax.shard_map(
        shards,
        mesh=mesh,
        in_specs=placed,
        out_specs=P("sec", "wide", "narrow", None),
        check_vma=False,
    )
```

```python
import math

import jax
import jax.numpy as jnp
from jax import lax
from jax.experimental import pallas as pl
from jax.experimental.pallas import tpu as pltpu
from jax.sharding import PartitionSpec as P

SEG = 16
SUBBAND_LIMIT = 2
TWO_PI = 2.0 * math.pi
VMEM_BYTES = 56 * 1024 * 1024
T_BLOCK = 8


def class_of_subbands(owners):
    sub_count = owners.shape[0]
    order = jnp.arange(sub_count, dtype=jnp.int32)
    mate = order + 1 - 2 * (order % 2)
    is_mate = mate[:, None] == order[None, :]
    mate_owner = jnp.sum(jnp.where(is_mate, owners[None, :], 0), axis=1)
    near = (mate_owner[:, None] == owners[None, :]) & ~is_mate
    near = near | near.T | (order[:, None] == order[None, :])
    reach = 1
    while reach < sub_count:
        step = near.astype(jnp.bfloat16)
        near = jnp.dot(step, step, preferred_element_type=jnp.float32) > 0.5
        reach *= 2
    least = jnp.min(jnp.where(near, order[None, :], sub_count), axis=1)
    least_of_mate = jnp.min(jnp.where(is_mate, least[None, :], sub_count), axis=1)
    return jnp.where(least < least_of_mate, 0, 1).astype(jnp.int32)


def filter_kernel(class_ref, volts_ref, taps_ref, table_ref, out_ref, frames, filtered, packed):
    source_count, group_size, rows, piece_len = volts_ref.shape
    tap_count, _, chan_count = taps_ref.shape
    block_count = 2
    pieces = source_count // block_count
    piece_frames = piece_len // chan_count
    frame_count = pieces * piece_frames
    station_count = table_ref.shape[0]
    pol_count = rows // (2 * station_count)
    frames[frame_count:] = jnp.zeros_like(frames[frame_count:])

    def one(index, carry):
        sub = index // block_count
        block = index % block_count
        for piece in range(pieces):
            for frame in range(piece_frames):
                frames[piece * piece_frames + frame] = volts_ref[
                    block * pieces + piece, sub, :, frame * chan_count : (frame + 1) * chan_count
                ].astype(jnp.float32)
        for low in range(0, chan_count, 128):
            lanes = slice(low, low + 128)
            taps = [taps_ref[tap, :, lanes] for tap in range(tap_count)]

            def some(step, inner):
                start = pl.multiple_of(step * T_BLOCK, T_BLOCK)
                loaded = [frames[start + i, :, lanes] for i in range(T_BLOCK + tap_count - 1)]
                for i in range(T_BLOCK):
                    total = taps[0] * loaded[i]
                    for tap in range(1, tap_count):
                        total = total + taps[tap] * loaded[i + tap]
                    at = pl.multiple_of((start + i) * rows, rows)
                    filtered[low // 128, pl.ds(at, rows), :] = total
                return inner

            lax.fori_loop(0, frame_count // T_BLOCK, some, 0)
        for station in range(station_count):
            parts = []
            for pol in range(pol_count):
                pair = [
                    filtered[
                        half,
                        pl.ds((station * pol_count + pol) * 2 + r, frame_count, stride=rows),
                        :,
                    ].astype(jnp.bfloat16)
                    for r in range(2)
                    for half in range(chan_count // 128)
                ]
                parts.append(jnp.concatenate(pair, axis=1))
            series = jnp.concatenate(parts, axis=0)
            spectra = lax.dot_general(
                table_ref[station],
                series,
                (((1,), (1,)), ((), ())),
                preferred_element_type=jnp.float32,
            )
            for r in range(2):
                for pol in range(pol_count):
                    packed[
                        block, pl.ds((station * 2 + r) * pol_count + pol, chan_count, stride=rows), :
                    ] = spectra[
                        r * chan_count : (r + 1) * chan_count,
                        pol * frame_count : (pol + 1) * frame_count,
                    ]

        @pl.when(block == block_count - 1)
        def _():
            for b in range(block_count):
                out_ref[class_ref[sub], :, :, b * frame_count : (b + 1) * frame_count] = (
                    packed[b].reshape(chan_count, rows, frame_count).astype(jnp.bfloat16)
                )

        return carry

    lax.fori_loop(0, group_size * block_count, one, 0)


def beam_kernel(spectra_ref, weights_ref, kern_ref, power_ref, held):
    source_count, chan_local, rows, length = spectra_ref.shape
    block_count, beam_count, block_len = power_ref.shape
    pol_count = 2
    depth = source_count * rows // pol_count
    span = 2 * SEG
    from_seg = lax.broadcasted_iota(jnp.int32, (block_len, block_len), 0) // SEG
    to_seg = lax.broadcasted_iota(jnp.int32, (block_len, block_len), 1) // SEG
    own_mask = (from_seg == to_seg) | (from_seg + 1 == to_seg)
    cross_mask = (from_seg == block_len // SEG - 1) & (to_seg == 0)
    power_ref[...] = jnp.zeros_like(power_ref)

    def one(chan, carry):
        for block in range(block_count):
            lanes = slice(block * block_len, (block + 1) * block_len)
            held[block] = (
                spectra_ref[:, chan, :, lanes]
                .astype(jnp.float32)
                .reshape(source_count * rows, block_len)
            )
        inputs = jnp.concatenate(
            [
                held[block, pl.ds(pol, depth, stride=pol_count), :].astype(jnp.bfloat16)
                for pol in range(pol_count)
                for block in range(block_count)
            ],
            axis=1,
        )
        beams = jnp.dot(
            weights_ref[chan], inputs, preferred_element_type=jnp.float32
        ).astype(jnp.bfloat16)
        tiled = [
            jnp.concatenate([kern_ref[chan, part]] * (block_len // span), axis=0)
            for part in range(2)
        ]

        def matrix(mask):
            real, imag = [jnp.where(mask, part, 0.0) for part in tiled]
            return jnp.concatenate(
                [
                    jnp.concatenate([real, imag], axis=1),
                    jnp.concatenate([-imag, real], axis=1),
                ],
                axis=0,
            ).astype(jnp.bfloat16)

        def series(block):
            parts = []
            for pol in range(pol_count):
                at = pol * length + block * block_len
                parts.append(
                    jnp.concatenate(
                        [
                            beams[:beam_count, at : at + block_len],
                            beams[beam_count:, at : at + block_len],
                        ],
                        axis=1,
                    )
                )
            return jnp.concatenate(parts, axis=0)

        own = matrix(own_mask)
        first, second = series(0), series(1)
        clean = [
            jnp.dot(first, own, preferred_element_type=jnp.float32),
            jnp.dot(second, own, preferred_element_type=jnp.float32)
            + jnp.dot(first, matrix(cross_mask), preferred_element_type=jnp.float32),
        ]
        for block in range(block_count):
            square = clean[block] * clean[block]
            both = square[:beam_count] + square[beam_count:]
            power_ref[block] += both[:, :block_len] + both[:, block_len:]
        return carry

    lax.fori_loop(0, chan_local, one, 0)


def shards(voltages, prototype, beam_delays, station_shifts, dm_index, owners):
    wide_count = lax.axis_size("wide")
    source_count = lax.axis_size("sec") * lax.axis_size("narrow")
    narrow_count = lax.axis_size("narrow")
    block_count = lax.axis_size("sec")
    _, sub_count, station_local, pol_count, _, piece_len = voltages.shape
    tap_count, chan_count = prototype.shape
    beam_count, station_count = beam_delays.shape
    rows = station_local * pol_count * 2
    group_size = sub_count // source_count
    chan_local = group_size * chan_count // wide_count
    chan_groups = chan_count // chan_local
    block_len = piece_len * narrow_count // chan_count
    length = block_count * block_len
    together = ("sec", "narrow")

    volts = voltages.reshape(sub_count, rows, piece_len)
    volts = lax.all_to_all(volts, together, 0, 0, tiled=True)
    volts = volts.reshape(source_count, group_size, rows, piece_len)

    flat = prototype.reshape(-1)
    taps = jnp.stack(
        [
            lax.dynamic_update_slice(
                jnp.zeros((tap_count + 1) * chan_count, jnp.float32), flat, (station_shifts[s],)
            ).reshape(tap_count + 1, chan_count)
            for s in range(station_local)
        ],
        axis=1,
    )
    taps = jnp.repeat(taps, 2 * pol_count, axis=1)
    ids = jnp.arange(chan_count, dtype=jnp.int32)
    turn = jnp.mod(
        ids[None, :, None] * (ids[None, None, :] - station_shifts[:, None, None]), chan_count
    )
    angle = turn.astype(jnp.float32) * (TWO_PI / chan_count)
    scale = 1.0 / math.sqrt(chan_count)
    cosine, sine = jnp.cos(angle) * scale, jnp.sin(angle) * scale
    table = jnp.concatenate(
        [
            jnp.concatenate([cosine, sine], axis=2),
            jnp.concatenate([-sine, cosine], axis=2),
        ],
        axis=1,
    ).astype(jnp.bfloat16)
    classes = class_of_subbands(owners)
    group = lax.axis_index("sec") * narrow_count + lax.axis_index("narrow")
    own_classes = lax.dynamic_slice_in_dim(classes, group * group_size, group_size)
    whole = pl.BlockSpec(memory_space=pltpu.VMEM)
    scalars = pl.BlockSpec(memory_space=pltpu.SMEM)
    spectra = pl.pallas_call(
        filter_kernel,
        out_shape=jax.ShapeDtypeStruct((group_size, chan_count, rows, length), jnp.bfloat16),
        in_specs=[scalars] + [whole] * 3,
        out_specs=whole,
        scratch_shapes=[
            pltpu.VMEM((block_len + tap_count, rows, chan_count), jnp.float32),
            pltpu.VMEM((chan_count // 128, block_len * rows, 128), jnp.float32),
            pltpu.VMEM((block_count, chan_count * rows, block_len), jnp.float32),
        ],
        compiler_params=pltpu.CompilerParams(vmem_limit_bytes=VMEM_BYTES),
        name="filter",
    )(own_classes, volts, taps, table)

    spectra = spectra.reshape(wide_count, chan_local, rows, length)
    spectra = lax.all_to_all(spectra, "wide", 0, 0, tiled=True)

    wide_index = lax.axis_index("wide")
    member = wide_index // chan_groups
    sub = group * group_size + jnp.where(own_classes[0] == member, 0, 1)
    channels = (wide_index % chan_groups) * chan_local + jnp.arange(chan_local, dtype=jnp.int32)

    frequency = sub.astype(jnp.float32) + channels.astype(jnp.float32) / chan_count
    delays = jnp.repeat(beam_delays, 2, axis=1)
    phase = (TWO_PI * frequency)[:, None, None] * delays[None]
    norm = 1.0 / math.sqrt(station_count)
    cosine, sine = jnp.cos(phase) * norm, jnp.sin(phase) * norm
    is_real = jnp.arange(2 * station_count)[None, None, :] % 2 == 0
    weights = jnp.concatenate(
        [jnp.where(is_real, cosine, sine), jnp.where(is_real, -sine, cosine)], axis=1
    ).astype(jnp.bfloat16)

    span = 2 * SEG
    bins = jnp.arange(span, dtype=jnp.int32)
    signed = jnp.where(bins < span // 2, bins, bins - span)
    dm_value = jnp.sum(jnp.where(jnp.arange(sub_count) == sub, dm_index, 0))
    phase_index = dm_value * signed[None, :] * (signed[None, :] + channels[:, None])
    angle_index = jnp.mod(
        phase_index[:, None, :] + 2 * bins[None, :, None] * bins[None, None, :], 2 * span
    )
    angles = angle_index.astype(jnp.float32) * (math.pi / span)
    kern = jnp.stack(
        [jnp.sum(jnp.cos(angles), axis=-1) / span, jnp.sum(jnp.sin(angles), axis=-1) / span],
        axis=1,
    ).astype(jnp.bfloat16)
    lag = jnp.mod(jnp.arange(block_len)[None, :] - bins[:, None], span)
    pick = (lag[None] == bins[:, None, None]).astype(jnp.bfloat16)
    kern = jnp.einsum("crd,dab->crab", kern, pick, preferred_element_type=jnp.float32)

    partial = pl.pallas_call(
        beam_kernel,
        out_shape=jax.ShapeDtypeStruct((block_count, beam_count, block_len), jnp.float32),
        in_specs=[whole] * 3,
        out_specs=whole,
        scratch_shapes=[pltpu.VMEM((block_count, wide_count * rows, block_len), jnp.float32)],
        compiler_params=pltpu.CompilerParams(vmem_limit_bytes=VMEM_BYTES),
        name="beams",
    )(spectra, weights, kern)

    partial = partial.reshape(source_count, beam_count // narrow_count, block_len)
    partial = lax.all_to_all(partial, together, 0, 0, tiled=True)
    order = jnp.arange(sub_count, dtype=jnp.int32)
    goes = (owners[None, :] == jnp.arange(wide_count)[:, None]) & (classes == member)[None, :]
    chosen = jnp.sum(jnp.where(goes, order[None, :] // group_size, 0), axis=1)
    outgoing = jnp.where(
        jnp.any(goes, axis=1)[:, None, None], jnp.take(partial, chosen, axis=0), 0.0
    )
    arrived = lax.all_to_all(outgoing, "wide", 0, 0, tiled=True)
    arrived = arrived.reshape(group_size, chan_groups, beam_count // narrow_count, block_len)
    by_class = jnp.sum(arrived, axis=1) / chan_count
    owned = owners == wide_index
    rank = jnp.cumsum(owned.astype(jnp.int32)) - 1
    shares = [
        [
            jnp.any(owned & (rank == slot) & (classes == which)).astype(jnp.float32)
            for which in range(group_size)
        ]
        for slot in range(SUBBAND_LIMIT)
    ]
    return jnp.stack(
        [sum(share * by_class[which] for which, share in enumerate(row)) for row in shares]
    )[None]


def solution(mesh):
    placed = (P("sec", None, "wide", None, None, "narrow"), P(), P(), P("wide"), P(), P())
    return jax.shard_map(
        shards,
        mesh=mesh,
        in_specs=placed,
        out_specs=P("sec", "wide", "narrow", None),
        check_vma=False,
    )
```

```python
import math

import jax
import jax.numpy as jnp
from jax import lax
from jax.experimental import pallas as pl
from jax.experimental.pallas import tpu as pltpu
from jax.sharding import PartitionSpec as P

SEG = 16
SUBBAND_LIMIT = 2
MAXD = 128
LEAD = 8
LANES = 128
TWO_PI = 2.0 * math.pi
VMEM_BYTES = 56 * 1024 * 1024


def filter_kernel(
    where_ref, own_ref, left_ref, right_ref, taps_ref, table_ref, out_ref, frames, filtered, packed
):
    sub_count, rows, piece_len = own_ref.shape
    tap_count, _, chan_count = taps_ref.shape
    station_count = table_ref.shape[0]
    pol_count = rows // (2 * station_count)
    quad = 2 * station_count
    spectra = piece_len // chan_count
    halves = chan_count // LANES
    width = pol_count * spectra
    fold = LANES // width
    members = filtered.shape[1] // (spectra * rows)
    fours = chan_count // fold
    zero = jnp.zeros((rows, LANES), jnp.float32)
    follows = jnp.where(where_ref[0] == 0, 0.0, 1.0)

    def one_batch(batch, carry):
        def one_sub(member, inner):
            sub = batch * members + member
            for half in range(halves):
                lanes = slice(half * LANES, half * LANES + LANES)
                taps = [taps_ref[tap, :, lanes] for tap in range(tap_count)]

                def load(ref, frame):
                    low = frame * chan_count + half * LANES
                    if low >= ref.shape[-1]:
                        return zero
                    return ref[sub, :, low : low + LANES].astype(jnp.float32)

                own = [load(own_ref, frame) for frame in range(spectra)]
                early = [load(left_ref, frame) for frame in range(LEAD)]
                early += [frame * follows for frame in own]
                late = own + [load(right_ref, frame) for frame in range(LEAD)]
                for number in range(spectra):
                    source = early[number:] if number < LEAD else late[number - LEAD :]
                    total = taps[0] * source[0]
                    for tap in range(1, tap_count):
                        total = total + taps[tap] * source[tap]
                    at = pl.multiple_of((member * spectra + number) * rows, rows)
                    filtered[half, pl.ds(at, rows), :] = total
            return inner

        lax.fori_loop(0, members, one_sub, 0)
        lane = lax.broadcasted_iota(jnp.int32, (fours, LANES), 1) // width
        for station in range(station_count):
            parts = []
            for member in range(members):
                for pol in range(pol_count):
                    first = member * spectra * rows + (station * pol_count + pol) * 2
                    parts.append(
                        jnp.concatenate(
                            [
                                filtered[half, pl.ds(first + r, spectra, stride=rows), :].astype(
                                    jnp.bfloat16
                                )
                                for r in range(2)
                                for half in range(halves)
                            ],
                            axis=1,
                        )
                    )
            spectrum = lax.dot_general(
                table_ref[station],
                jnp.concatenate(parts, axis=0),
                (((1,), (1,)), ((), ())),
                preferred_element_type=jnp.float32,
            )
            for r in range(2):
                for tile in range(members // fold):
                    blocks = [
                        spectrum[
                            (r * fold + turn) * fours : (r * fold + turn + 1) * fours,
                            tile * LANES : (tile + 1) * LANES,
                        ]
                        for turn in range(fold)
                    ]
                    for member in range(fold):
                        whole = None
                        for turn, block in enumerate(blocks):
                            shift = (turn - member) * width % LANES
                            moved = pltpu.roll(block, shift, 1) if shift else block
                            whole = moved if whole is None else jnp.where(lane == turn, moved, whole)
                        packed[
                            tile * fold + member,
                            pl.ds(station * 2 + r, fours, stride=quad),
                            :,
                        ] = whole
        for member in range(members):
            out_ref[batch * members + member] = packed[member].astype(jnp.bfloat16)
        return carry

    lax.fori_loop(0, sub_count // members, one_batch, 0)


def beam_kernel(
    spectra_ref, tail_ref, weights_ref, kern_ref, order_ref, power_ref, held, held_tail, total
):
    source_count, piece_count, row_count, _ = spectra_ref.shape
    beam_count, block_len = power_ref.shape
    chan_local = weights_ref.shape[0]
    pol_count = 2
    spectra = block_len // piece_count
    width = pol_count * spectra
    fold = LANES // width
    quad = row_count * fold // chan_local
    step_rows = 8
    span = 2 * SEG
    from_time = lax.broadcasted_iota(jnp.int32, (block_len, block_len), 0)
    to_time = lax.broadcasted_iota(jnp.int32, (block_len, block_len), 1)
    from_seg = lax.rem(from_time + block_len - LEAD, block_len) // SEG
    to_seg = lax.rem(to_time + block_len - LEAD, block_len) // SEG
    own_mask = (from_seg == to_seg) | (from_seg + 1 == to_seg)
    cross_mask = to_seg[:spectra] == 0
    no_rows = jnp.zeros((block_len - spectra, block_len), jnp.float32)
    lane = lax.broadcasted_iota(jnp.int32, (source_count * quad, block_len), 1) // spectra
    total[...] = jnp.zeros_like(total)

    def gathered(ref, inner):
        return jnp.concatenate(
            [ref[pl.ds(inner * quad + q, source_count, stride=step_rows), :] for q in range(quad)],
            axis=0,
        )

    def turned(value, shift):
        return pltpu.roll(value, shift % LANES, 1) if shift % LANES else value

    def matrix(real, imag):
        return jnp.concatenate(
            [jnp.concatenate([real, imag], axis=1), jnp.concatenate([-imag, real], axis=1)], axis=0
        ).astype(jnp.bfloat16)

    def one(step, carry):
        at = pl.multiple_of(step * step_rows, step_rows)
        shape = (source_count * step_rows, LANES)
        for piece in range(piece_count):
            held[piece] = (
                spectra_ref[:, piece, pl.ds(at, step_rows), :].astype(jnp.float32).reshape(shape)
            )
        held_tail[...] = tail_ref[:, pl.ds(at, step_rows), :].astype(jnp.float32).reshape(shape)
        for inner in range(step_rows // quad):
            pieces = [gathered(held.at[piece], inner) for piece in range(piece_count)]
            tail = gathered(held_tail, inner)
            for turn in range(fold):
                chan = step * (step_rows // quad * fold) + inner * fold + turn
                parts = []
                for pol in range(pol_count):
                    low = turn * width + pol * spectra
                    whole = turned(pieces[0], -low)
                    for piece in range(1, piece_count):
                        moved = turned(pieces[piece], piece * spectra - low)
                        whole = jnp.where(lane == piece, moved, whole)
                    parts.append(whole.astype(jnp.bfloat16))
                for pol in range(pol_count):
                    parts.append(
                        turned(tail, -(turn * width + pol * spectra)).astype(jnp.bfloat16)
                    )
                beams = jnp.dot(
                    weights_ref[chan],
                    jnp.concatenate(parts, axis=1),
                    preferred_element_type=jnp.float32,
                ).astype(jnp.bfloat16)

                def series(first):
                    return jnp.concatenate(
                        [
                            jnp.concatenate(
                                [
                                    beams[
                                        part * beam_count : (part + 1) * beam_count,
                                        (first + pol) * LANES : (first + pol + 1) * LANES,
                                    ]
                                    for part in range(2)
                                ],
                                axis=1,
                            )
                            for pol in range(pol_count)
                        ],
                        axis=0,
                    )

                kern = [kern_ref[chan, part] for part in range(2)]
                own = [
                    jnp.where(own_mask, jnp.concatenate([part] * (block_len // span), axis=0), 0.0)
                    for part in kern
                ]
                cross = [
                    jnp.concatenate(
                        [
                            jnp.where(
                                cross_mask,
                                jnp.concatenate([part[:LEAD], part[span - LEAD :]], axis=0),
                                0.0,
                            ),
                            no_rows,
                        ],
                        axis=0,
                    )
                    for part in kern
                ]
                clean = jnp.dot(
                    series(0), matrix(*own), preferred_element_type=jnp.float32
                ) + jnp.dot(
                    series(pol_count), matrix(*cross), preferred_element_type=jnp.float32
                )
                square = clean * clean
                both = square[:beam_count] + square[beam_count:]
                total[...] += both[:, :block_len] + both[:, block_len:]
        return carry

    lax.fori_loop(0, row_count // step_rows, one, 0)
    power_ref[...] = jnp.dot(
        total[...],
        order_ref[...],
        precision=lax.Precision.HIGHEST,
        preferred_element_type=jnp.float32,
    )


def shards(voltages, prototype, beam_delays, station_shifts, dm_index, owners):
    wide_count = lax.axis_size("wide")
    narrow_count = lax.axis_size("narrow")
    wide_index = lax.axis_index("wide")
    narrow_index = lax.axis_index("narrow")
    _, sub_count, station_local, pol_count, _, piece_len = voltages.shape
    tap_count, chan_count = prototype.shape
    beam_count, station_count = beam_delays.shape
    rows = station_local * pol_count * 2
    quad = station_local * 2
    spectra = piece_len // chan_count
    block_len = spectra * narrow_count
    chan_local = chan_count // narrow_count
    fold = LANES // (pol_count * spectra)
    fours = chan_count // fold
    members = min(2 * fold, sub_count)
    whole = pl.BlockSpec(memory_space=pltpu.VMEM)
    scalars = pl.BlockSpec(memory_space=pltpu.SMEM)
    params = pltpu.CompilerParams(vmem_limit_bytes=VMEM_BYTES)

    volts = voltages.reshape(sub_count, rows, piece_len)
    ahead = (tap_count - 1 - LEAD) * chan_count + MAXD
    right = lax.ppermute(
        volts[..., :ahead], "narrow", [(i, i - 1) for i in range(1, narrow_count)]
    )
    left = lax.ppermute(
        volts[..., piece_len - LEAD * chan_count :],
        "narrow",
        [(i, (i + 1) % narrow_count) for i in range(narrow_count)],
    )

    flat = prototype.reshape(-1)
    taps = jnp.stack(
        [
            lax.dynamic_update_slice(
                jnp.zeros((tap_count + 1) * chan_count, jnp.float32), flat, (station_shifts[s],)
            ).reshape(tap_count + 1, chan_count)
            for s in range(station_local)
        ],
        axis=1,
    )
    taps = jnp.repeat(taps, 2 * pol_count, axis=1)
    ids = jnp.arange(chan_count, dtype=jnp.int32)
    row_chan = (ids % fours) * fold + ids // fours
    turn = jnp.mod(
        row_chan[None, :, None] * (ids[None, None, :] - station_shifts[:, None, None]), chan_count
    )
    angle = turn.astype(jnp.float32) * (TWO_PI / chan_count)
    scale = 1.0 / math.sqrt(chan_count)
    cosine, sine = jnp.cos(angle) * scale, jnp.sin(angle) * scale
    table = jnp.concatenate(
        [
            jnp.concatenate([cosine, sine], axis=2),
            jnp.concatenate([-sine, cosine], axis=2),
        ],
        axis=1,
    ).astype(jnp.bfloat16)
    packed = pl.pallas_call(
        filter_kernel,
        out_shape=jax.ShapeDtypeStruct((sub_count, fours * quad, LANES), jnp.bfloat16),
        in_specs=[scalars] + [whole] * 5,
        out_specs=whole,
        scratch_shapes=[
            pltpu.VMEM((8, LANES), jnp.float32),
            pltpu.VMEM((chan_count // LANES, members * spectra * rows, LANES), jnp.float32),
            pltpu.VMEM((members, fours * quad, LANES), jnp.float32),
        ],
        compiler_params=params,
        name="filter",
    )(narrow_index.astype(jnp.int32)[None], volts, left, right, taps, table)

    local_rows = fours * quad // narrow_count
    packed = packed.reshape(sub_count * narrow_count, local_rows, LANES)
    packed = lax.all_to_all(packed, ("wide", "narrow"), 0, 0, tiled=True)
    packed = packed.reshape(wide_count, narrow_count, local_rows, LANES)

    early = jnp.arange(LANES) % spectra < LEAD
    tail = jnp.where(early, packed[:, 0], packed[:, narrow_count - 1])
    tail = lax.ppermute(tail, "sec", [(0, 1)])

    sub = wide_index
    channels = narrow_index * chan_local + jnp.arange(chan_local, dtype=jnp.int32)
    frequency = sub.astype(jnp.float32) + channels.astype(jnp.float32) / chan_count
    delays = jnp.transpose(beam_delays.reshape(beam_count, wide_count, station_local), (0, 2, 1))
    delays = jnp.repeat(delays, 2, axis=1).reshape(beam_count, 2 * station_count)
    phase = (TWO_PI * frequency)[:, None, None] * delays[None]
    norm = 1.0 / math.sqrt(station_count)
    cosine, sine = jnp.cos(phase) * norm, jnp.sin(phase) * norm
    is_real = jnp.arange(2 * station_count)[None, None, :] // wide_count % 2 == 0
    weights = jnp.concatenate(
        [jnp.where(is_real, cosine, sine), jnp.where(is_real, -sine, cosine)], axis=1
    ).astype(jnp.bfloat16)

    span = 2 * SEG
    bins = jnp.arange(span, dtype=jnp.int32)
    signed = jnp.where(bins < span // 2, bins, bins - span)
    dm_value = jnp.sum(jnp.where(jnp.arange(sub_count) == sub, dm_index, 0))
    phase_index = dm_value * signed[None, :] * (signed[None, :] + channels[:, None])
    angle_index = jnp.mod(
        phase_index[:, None, :] + 2 * bins[None, :, None] * bins[None, None, :], 2 * span
    )
    angles = angle_index.astype(jnp.float32) * (math.pi / span)
    kern = jnp.stack(
        [jnp.sum(jnp.cos(angles), axis=-1) / span, jnp.sum(jnp.sin(angles), axis=-1) / span],
        axis=1,
    ).astype(jnp.bfloat16)
    times = jnp.arange(block_len, dtype=jnp.int32)
    lag = jnp.mod(times[None, :] - bins[:, None], span)
    pick = (lag[None] == bins[:, None, None]).astype(jnp.bfloat16)
    kern = jnp.einsum("crd,dab->crab", kern, pick, preferred_element_type=jnp.float32)
    order = (jnp.mod(times - LEAD, block_len)[:, None] == times[None, :]).astype(jnp.float32)

    partial = pl.pallas_call(
        beam_kernel,
        out_shape=jax.ShapeDtypeStruct((beam_count, block_len), jnp.float32),
        in_specs=[whole] * 5,
        out_specs=whole,
        scratch_shapes=[
            pltpu.VMEM((narrow_count, wide_count * 8, LANES), jnp.float32),
            pltpu.VMEM((wide_count * 8, LANES), jnp.float32),
            pltpu.VMEM((beam_count, block_len), jnp.float32),
        ],
        compiler_params=params,
        name="beams",
    )(packed, tail, weights, kern, order)

    partial = partial.reshape(narrow_count, beam_count // narrow_count, block_len)
    partial = lax.all_to_all(partial, "narrow", 0, 0, tiled=True)
    share = jnp.sum(partial, axis=0) / chan_count
    subs = jnp.arange(sub_count, dtype=jnp.int32)
    owner = jnp.sum(jnp.where(subs == sub, owners, 0))
    goes = jnp.arange(wide_count, dtype=jnp.int32) == owner
    outgoing = jnp.where(goes[:, None, None], share[None], 0.0)
    arrived = lax.all_to_all(outgoing, "wide", 0, 0, tiled=True)
    owned = owners == wide_index
    rank = jnp.cumsum(owned.astype(jnp.int32)) - 1
    slots = jnp.arange(SUBBAND_LIMIT, dtype=jnp.int32)
    held = owned[None, :] & (rank[None, :] == slots[:, None])
    chosen = jnp.sum(jnp.where(held, subs[None, :], 0), axis=1)
    result = jnp.take(arrived, chosen, axis=0)
    return jnp.where(jnp.any(held, axis=1)[:, None, None], result, 0.0)[None]


def solution(mesh):
    placed = (P("sec", None, "wide", None, None, "narrow"), P(), P(), P("wide"), P(), P())
    return jax.shard_map(
        shards,
        mesh=mesh,
        in_specs=placed,
        out_specs=P("sec", "wide", "narrow", None),
        check_vma=False,
    )
```

```python
import math

import jax
import jax.numpy as jnp
from jax import lax
from jax.experimental import pallas as pl
from jax.experimental.pallas import tpu as pltpu
from jax.sharding import PartitionSpec as P

SEG = 16
SUBBAND_LIMIT = 2
MAXD = 128
LEAD = 8
LANES = 128
TWO_PI = 2.0 * math.pi
UNROLL = 2
SHARES = 2
VMEM_BYTES = 56 * 1024 * 1024


def filter_kernel(
    where_ref, own_ref, left_ref, right_ref, taps_ref, table_ref, *refs
):
    out_ref, filtered, packed = refs[-3:]
    members, rows, piece_len = own_ref.shape
    tap_count, _, chan_count = taps_ref.shape
    station_count = table_ref.shape[0]
    pol_count = rows // (2 * station_count)
    quad = 2 * station_count
    spectra = piece_len // chan_count
    halves = chan_count // LANES
    width = pol_count * spectra
    fold = LANES // width
    fours = chan_count // fold
    zero = jnp.zeros((rows, LANES), jnp.float32)
    follows = jnp.where(where_ref[0] == 0, 0.0, 1.0)

    def one_sub(member, inner):
        for half in range(halves):
            lanes = slice(half * LANES, half * LANES + LANES)
            taps = [taps_ref[tap, :, lanes] for tap in range(tap_count)]

            def load(ref, frame):
                low = frame * chan_count + half * LANES
                if low >= ref.shape[-1]:
                    return zero
                return ref[member, :, low : low + LANES].astype(jnp.float32)

            own = [load(own_ref, frame) for frame in range(spectra)]
            early = [load(left_ref, frame) for frame in range(LEAD)]
            early += [frame * follows for frame in own]
            late = own + [load(right_ref, frame) for frame in range(LEAD)]
            for number in range(spectra):
                source = early[number:] if number < LEAD else late[number - LEAD :]
                total = taps[0] * source[0]
                for tap in range(1, tap_count):
                    total = total + taps[tap] * source[tap]
                at = pl.multiple_of((member * spectra + number) * rows, rows)
                filtered[half, pl.ds(at, rows), :] = total
        return inner

    lax.fori_loop(0, members, one_sub, 0)
    lane = lax.broadcasted_iota(jnp.int32, (fours, LANES), 1) // width
    for station in range(station_count):
        parts = []
        for member in range(members):
            for pol in range(pol_count):
                first = member * spectra * rows + (station * pol_count + pol) * 2
                parts.append(
                    jnp.concatenate(
                        [
                            filtered[half, pl.ds(first + r, spectra, stride=rows), :].astype(
                                jnp.bfloat16
                            )
                            for r in range(2)
                            for half in range(halves)
                        ],
                        axis=1,
                    )
                )
        spectrum = lax.dot_general(
            table_ref[station],
            jnp.concatenate(parts, axis=0),
            (((1,), (1,)), ((), ())),
            preferred_element_type=jnp.float32,
        )
        for r in range(2):
            for tile in range(members // fold):
                blocks = [
                    spectrum[
                        (r * fold + turn) * fours : (r * fold + turn + 1) * fours,
                        tile * LANES : (tile + 1) * LANES,
                    ]
                    for turn in range(fold)
                ]
                step = fold // 2
                while step:
                    low = (lane // step) % 2 == 0
                    swapped = list(blocks)
                    for first in range(fold):
                        if first // step % 2 == 0:
                            a, b = blocks[first], blocks[first + step]
                            swapped[first] = jnp.where(low, a, pltpu.roll(b, step * width, 1))
                            swapped[first + step] = jnp.where(
                                low, pltpu.roll(a, LANES - step * width, 1), b
                            )
                    blocks = swapped
                    step //= 2
                for member, block in enumerate(blocks):
                    packed[tile * fold + member, :, station * 2 + r] = block.reshape(
                        fours // 8, 8, LANES
                    )
    for member in range(members):
        out_ref[member] = packed[member].reshape(fours * quad, LANES).astype(jnp.bfloat16)


def beam_kernel(
    spectra_ref, tail_ref, weights_ref, kern_ref, order_ref, power_ref, held, held_tail, total
):
    source_count, piece_count, row_count, _ = spectra_ref.shape
    beam_count, block_len = power_ref.shape
    chan_local = weights_ref.shape[0]
    pol_count = 2
    spectra = block_len // piece_count
    width = pol_count * spectra
    fold = LANES // width
    quad = row_count * fold // chan_local
    eight = row_count // quad
    span = 2 * SEG
    from_time = lax.broadcasted_iota(jnp.int32, (block_len, block_len), 0)
    to_time = lax.broadcasted_iota(jnp.int32, (block_len, block_len), 1)
    from_seg = lax.rem(from_time + block_len - LEAD, block_len) // SEG
    to_seg = lax.rem(to_time + block_len - LEAD, block_len) // SEG
    own_mask = (from_seg == to_seg) | (from_seg + 1 == to_seg)
    cross_mask = to_seg[:spectra] == 0
    no_rows = jnp.zeros((block_len - spectra, block_len), jnp.float32)
    lane = lax.broadcasted_iota(jnp.int32, (source_count * quad, block_len), 1) // spectra
    total[...] = jnp.zeros_like(total)

    def gathered(ref, number):
        return jnp.concatenate(
            [
                ref[pl.ds(q * eight + number, source_count, stride=row_count), :]
                for q in range(quad)
            ],
            axis=0,
        )

    def turned(value, shift):
        return pltpu.roll(value, shift % LANES, 1) if shift % LANES else value

    def matrix(real, imag):
        return jnp.concatenate(
            [jnp.concatenate([real, imag], axis=1), jnp.concatenate([-imag, real], axis=1)], axis=0
        ).astype(jnp.bfloat16)

    shape = (source_count * row_count, LANES)
    for piece in range(piece_count):
        held[piece] = spectra_ref[:, piece].astype(jnp.float32).reshape(shape)
    held_tail[...] = tail_ref[...].astype(jnp.float32).reshape(shape)

    def one(step, carry):
        for inner in range(UNROLL):
            number = step * UNROLL + inner
            pieces = [gathered(held.at[piece], number) for piece in range(piece_count)]
            tail = gathered(held_tail, number)
            for turn in range(fold):
                chan = number * fold + turn
                parts = []
                for pol in range(pol_count):
                    low = turn * width + pol * spectra
                    whole = turned(pieces[0], -low)
                    for piece in range(1, piece_count):
                        moved = turned(pieces[piece], piece * spectra - low)
                        whole = jnp.where(lane == piece, moved, whole)
                    parts.append(whole.astype(jnp.bfloat16))
                for pol in range(pol_count):
                    parts.append(
                        turned(tail, -(turn * width + pol * spectra)).astype(jnp.bfloat16)
                    )
                beams = jnp.dot(
                    weights_ref[chan],
                    jnp.concatenate(parts, axis=1),
                    preferred_element_type=jnp.float32,
                ).astype(jnp.bfloat16)

                def series(first):
                    return jnp.concatenate(
                        [
                            jnp.concatenate(
                                [
                                    beams[
                                        part * beam_count : (part + 1) * beam_count,
                                        (first + pol) * LANES : (first + pol + 1) * LANES,
                                    ]
                                    for part in range(2)
                                ],
                                axis=1,
                            )
                            for pol in range(pol_count)
                        ],
                        axis=0,
                    )

                kern = [kern_ref[chan, part] for part in range(2)]
                own = [
                    jnp.where(own_mask, jnp.concatenate([part] * (block_len // span), axis=0), 0.0)
                    for part in kern
                ]
                cross = [
                    jnp.concatenate(
                        [
                            jnp.where(
                                cross_mask,
                                jnp.concatenate([part[:LEAD], part[span - LEAD :]], axis=0),
                                0.0,
                            ),
                            no_rows,
                        ],
                        axis=0,
                    )
                    for part in kern
                ]
                clean = jnp.dot(
                    series(0), matrix(*own), preferred_element_type=jnp.float32
                ) + jnp.dot(
                    series(pol_count), matrix(*cross), preferred_element_type=jnp.float32
                )
                square = clean * clean
                both = square[:beam_count] + square[beam_count:]
                total[...] += both[:, :block_len] + both[:, block_len:]
        return carry

    lax.fori_loop(0, eight // UNROLL, one, 0)
    power_ref[...] = jnp.dot(
        total[...],
        order_ref[...],
        precision=lax.Precision.HIGHEST,
        preferred_element_type=jnp.float32,
    )


def shards(voltages, prototype, beam_delays, station_shifts, dm_index, owners):
    wide_count = lax.axis_size("wide")
    narrow_count = lax.axis_size("narrow")
    wide_index = lax.axis_index("wide")
    narrow_index = lax.axis_index("narrow")
    _, sub_count, station_local, pol_count, _, piece_len = voltages.shape
    tap_count, chan_count = prototype.shape
    beam_count, station_count = beam_delays.shape
    rows = station_local * pol_count * 2
    quad = station_local * 2
    spectra = piece_len // chan_count
    block_len = spectra * narrow_count
    chan_local = chan_count // narrow_count
    fold = LANES // (pol_count * spectra)
    fours = chan_count // fold
    members = min(2 * fold, sub_count // SHARES)
    whole = pl.BlockSpec(memory_space=pltpu.VMEM)
    scalars = pl.BlockSpec(memory_space=pltpu.SMEM)
    params = pltpu.CompilerParams(vmem_limit_bytes=VMEM_BYTES)

    volts = voltages.reshape(sub_count, rows, piece_len)
    ahead = (tap_count - 1 - LEAD) * chan_count + MAXD
    share = sub_count // SHARES
    ends = [
        (
            lax.ppermute(
                volts[i * share : (i + 1) * share, :, piece_len - LEAD * chan_count :],
                "narrow",
                [(i, (i + 1) % narrow_count) for i in range(narrow_count)],
            ),
            lax.ppermute(
                volts[i * share : (i + 1) * share, :, :ahead],
                "narrow",
                [(i, i - 1) for i in range(1, narrow_count)],
            ),
        )
        for i in range(SHARES)
    ]

    flat = prototype.reshape(-1)
    taps = jnp.stack(
        [
            lax.dynamic_update_slice(
                jnp.zeros((tap_count + 1) * chan_count, jnp.float32), flat, (station_shifts[s],)
            ).reshape(tap_count + 1, chan_count)
            for s in range(station_local)
        ],
        axis=1,
    )
    taps = jnp.repeat(taps, 2 * pol_count, axis=1)
    ids = jnp.arange(chan_count, dtype=jnp.int32)
    row_chan = (ids % fours) * fold + ids // fours
    turn = jnp.mod(
        row_chan[None, :, None] * (ids[None, None, :] - station_shifts[:, None, None]), chan_count
    )
    angle = turn.astype(jnp.float32) * (TWO_PI / chan_count)
    scale = 1.0 / math.sqrt(chan_count)
    cosine, sine = jnp.cos(angle) * scale, jnp.sin(angle) * scale
    table = jnp.concatenate(
        [
            jnp.concatenate([cosine, sine], axis=2),
            jnp.concatenate([-sine, cosine], axis=2),
        ],
        axis=1,
    ).astype(jnp.bfloat16)
    packed = None
    for i, (left, right) in enumerate(ends):
        steps = share // members

        def block(length, first):
            return pl.BlockSpec((members, rows, length), lambda step: (step + first, 0, 0))

        packed = pl.pallas_call(
            filter_kernel,
            grid=(steps,),
            out_shape=jax.ShapeDtypeStruct((sub_count, fours * quad, LANES), jnp.bfloat16),
            in_specs=[
                scalars,
                block(piece_len, i * steps),
                block(LEAD * chan_count, 0),
                block(ahead, 0),
                whole,
                whole,
            ]
            + [pl.BlockSpec(memory_space=pl.ANY)] * min(i, 1),
            out_specs=pl.BlockSpec(
                (members, fours * quad, LANES), lambda step, first=i * steps: (step + first, 0, 0)
            ),
            scratch_shapes=[
                pltpu.VMEM((chan_count // LANES, members * spectra * rows, LANES), jnp.float32),
                pltpu.VMEM((members, fours // 8, quad, 8, LANES), jnp.float32),
            ],
            input_output_aliases={6: 0} if i else {},
            compiler_params=params,
            name="filter",
        )(
            narrow_index.astype(jnp.int32)[None],
            volts,
            left,
            right,
            taps,
            table,
            *([packed] if i else []),
        )

    local_rows = fours * quad // narrow_count
    packed = packed.reshape(sub_count * narrow_count, local_rows, LANES)
    packed = lax.all_to_all(packed, ("wide", "narrow"), 0, 0, tiled=True)
    packed = packed.reshape(wide_count, narrow_count, local_rows, LANES)

    early = jnp.arange(LANES) % spectra < LEAD
    tail = jnp.where(early, packed[:, 0], packed[:, narrow_count - 1])
    tail = lax.ppermute(tail, "sec", [(0, 1)])

    sub = wide_index
    channels = narrow_index * chan_local + jnp.arange(chan_local, dtype=jnp.int32)
    frequency = sub.astype(jnp.float32) + channels.astype(jnp.float32) / chan_count
    delays = jnp.transpose(beam_delays.reshape(beam_count, wide_count, station_local), (0, 2, 1))
    delays = jnp.repeat(delays, 2, axis=1).reshape(beam_count, 2 * station_count)
    phase = (TWO_PI * frequency)[:, None, None] * delays[None]
    norm = 1.0 / math.sqrt(station_count)
    cosine, sine = jnp.cos(phase) * norm, jnp.sin(phase) * norm
    is_real = jnp.arange(2 * station_count)[None, None, :] // wide_count % 2 == 0
    weights = jnp.concatenate(
        [jnp.where(is_real, cosine, sine), jnp.where(is_real, -sine, cosine)], axis=1
    ).astype(jnp.bfloat16)

    span = 2 * SEG
    bins = jnp.arange(span, dtype=jnp.int32)
    signed = jnp.where(bins < span // 2, bins, bins - span)
    dm_value = jnp.sum(jnp.where(jnp.arange(sub_count) == sub, dm_index, 0))
    phase_index = dm_value * signed[None, :] * (signed[None, :] + channels[:, None])
    angle_index = jnp.mod(
        phase_index[:, None, :] + 2 * bins[None, :, None] * bins[None, None, :], 2 * span
    )
    angles = angle_index.astype(jnp.float32) * (math.pi / span)
    kern = jnp.stack(
        [jnp.sum(jnp.cos(angles), axis=-1) / span, jnp.sum(jnp.sin(angles), axis=-1) / span],
        axis=1,
    ).astype(jnp.bfloat16)
    times = jnp.arange(block_len, dtype=jnp.int32)
    lag = jnp.mod(times[None, :] - bins[:, None], span)
    pick = (lag[None] == bins[:, None, None]).astype(jnp.bfloat16)
    kern = jnp.einsum("crd,dab->crab", kern, pick, preferred_element_type=jnp.float32)
    order = (jnp.mod(times - LEAD, block_len)[:, None] == times[None, :]).astype(jnp.float32)

    partial = pl.pallas_call(
        beam_kernel,
        out_shape=jax.ShapeDtypeStruct((beam_count, block_len), jnp.float32),
        in_specs=[whole] * 5,
        out_specs=whole,
        scratch_shapes=[
            pltpu.VMEM((narrow_count, wide_count * local_rows, LANES), jnp.float32),
            pltpu.VMEM((wide_count * local_rows, LANES), jnp.float32),
            pltpu.VMEM((beam_count, block_len), jnp.float32),
        ],
        compiler_params=params,
        name="beams",
    )(packed, tail, weights, kern, order)

    partial = partial.reshape(narrow_count, beam_count // narrow_count, block_len)
    partial = lax.all_to_all(partial, "narrow", 0, 0, tiled=True)
    summed = jnp.sum(partial, axis=0) / chan_count
    subs = jnp.arange(sub_count, dtype=jnp.int32)
    owner = jnp.sum(jnp.where(subs == sub, owners, 0))
    goes = jnp.arange(wide_count, dtype=jnp.int32) == owner
    outgoing = jnp.where(goes[:, None, None], summed[None], 0.0)
    arrived = lax.all_to_all(outgoing, "wide", 0, 0, tiled=True)
    owned = owners == wide_index
    rank = jnp.cumsum(owned.astype(jnp.int32)) - 1
    slots = jnp.arange(SUBBAND_LIMIT, dtype=jnp.int32)
    held = owned[None, :] & (rank[None, :] == slots[:, None])
    chosen = jnp.sum(jnp.where(held, subs[None, :], 0), axis=1)
    result = jnp.take(arrived, chosen, axis=0)
    return jnp.where(jnp.any(held, axis=1)[:, None, None], result, 0.0)[None]


def solution(mesh):
    placed = (P("sec", None, "wide", None, None, "narrow"), P(), P(), P("wide"), P(), P())
    return jax.shard_map(
        shards,
        mesh=mesh,
        in_specs=placed,
        out_specs=P("sec", "wide", "narrow", None),
        check_vma=False,
    )
```

```python
import math

import jax
import jax.numpy as jnp
from jax import lax
from jax.experimental import pallas as pl
from jax.experimental.pallas import tpu as pltpu
from jax.sharding import PartitionSpec as P

SEG = 16
SUBBAND_LIMIT = 2
MAXD = 128
LEAD = 8
LANES = 128
TWO_PI = 2.0 * math.pi
UNROLL = 4
PITCH = 40
SHARES = 2
FILTER_VMEM = 63 * 1024 * 1024
VMEM_BYTES = 48 * 1024 * 1024


def filter_kernel(
    where_ref, shifts_ref, own_ref, left_ref, right_ref, prototype_ref, table_ref, *refs
):
    out_ref, taps_ref, filtered, packed = refs[-4:]
    members, rows, piece_len = own_ref.shape
    tap_count, _, chan_count = taps_ref.shape
    station_count = table_ref.shape[0]
    pol_count = rows // (2 * station_count)
    quad = 2 * station_count
    spectra = piece_len // chan_count
    halves = chan_count // LANES
    width = pol_count * spectra
    fold = LANES // width
    fours = chan_count // fold
    zero = jnp.zeros((rows, LANES), jnp.float32)

    @pl.when(pl.program_id(0) == 0)
    def _():
        lane = lax.broadcasted_iota(jnp.int32, prototype_ref.shape[1:], 1)
        moved = [
            jnp.where(
                lane < shifts_ref[station],
                pltpu.roll(prototype_ref[1], shifts_ref[station], 1),
                pltpu.roll(prototype_ref[0], shifts_ref[station], 1),
            )
            for station in range(station_count)
        ]
        row = lax.broadcasted_iota(jnp.int32, (rows, chan_count), 0) // (2 * pol_count)
        for tap in range(tap_count):
            whole = jnp.broadcast_to(moved[0][tap : tap + 1], (rows, chan_count))
            for station in range(1, station_count):
                other = jnp.broadcast_to(moved[station][tap : tap + 1], (rows, chan_count))
                whole = jnp.where(row == station, other, whole)
            taps_ref[tap] = whole

    follows = jnp.where(where_ref[0] == 0, 0.0, 1.0)

    def one_sub(member, inner):
        for half in range(halves):
            lanes = slice(half * LANES, half * LANES + LANES)
            taps = [taps_ref[tap, :, lanes] for tap in range(tap_count)]

            def load(ref, frame):
                low = frame * chan_count + half * LANES
                if low >= ref.shape[-1]:
                    return zero
                return ref[member, :, low : low + LANES].astype(jnp.float32)

            own = [load(own_ref, frame) for frame in range(spectra)]
            early = [load(left_ref, frame) for frame in range(LEAD)]
            early += [frame * follows for frame in own]
            late = own + [load(right_ref, frame) for frame in range(LEAD)]
            for number in range(spectra):
                source = early[number:] if number < LEAD else late[number - LEAD :]
                total = taps[0] * source[0]
                for tap in range(1, tap_count):
                    total = total + taps[tap] * source[tap]
                at = pl.multiple_of((member * spectra + number) * rows, rows)
                filtered[half, pl.ds(at, rows), :] = total
        return inner

    lax.fori_loop(0, members, one_sub, 0)
    lane = lax.broadcasted_iota(jnp.int32, (fours, LANES), 1) // width
    for station in range(station_count):
        parts = []
        for member in range(members):
            for pol in range(pol_count):
                first = member * spectra * rows + (station * pol_count + pol) * 2
                parts.append(
                    jnp.concatenate(
                        [
                            filtered[half, pl.ds(first + r, spectra, stride=rows), :].astype(
                                jnp.bfloat16
                            )
                            for r in range(2)
                            for half in range(halves)
                        ],
                        axis=1,
                    )
                )
        spectrum = lax.dot_general(
            table_ref[station],
            jnp.concatenate(parts, axis=0),
            (((1,), (1,)), ((), ())),
            preferred_element_type=jnp.float32,
        )
        for r in range(2):
            for tile in range(members // fold):
                blocks = [
                    spectrum[
                        (r * fold + turn) * fours : (r * fold + turn + 1) * fours,
                        tile * LANES : (tile + 1) * LANES,
                    ]
                    for turn in range(fold)
                ]
                step = fold // 2
                while step:
                    low = (lane // step) % 2 == 0
                    swapped = list(blocks)
                    for first in range(fold):
                        if first // step % 2 == 0:
                            a, b = blocks[first], blocks[first + step]
                            swapped[first] = jnp.where(low, a, pltpu.roll(b, step * width, 1))
                            swapped[first + step] = jnp.where(
                                low, pltpu.roll(a, LANES - step * width, 1), b
                            )
                    blocks = swapped
                    step //= 2
                for member, block in enumerate(blocks):
                    packed[tile * fold + member, :, station * 2 + r] = block.reshape(
                        fours // 8, 8, LANES
                    )
    for member in range(members):
        out_ref[member] = packed[member].reshape(fours * quad, LANES).astype(jnp.bfloat16)


def beam_kernel(
    spectra_ref, tail_ref, weights_ref, kern_ref, order_ref, power_ref, held, held_tail, total
):
    source_count, piece_count, row_count, _ = spectra_ref.shape
    beam_count, block_len = power_ref.shape
    chan_local = weights_ref.shape[0]
    pol_count = 2
    spectra = block_len // piece_count
    width = pol_count * spectra
    fold = LANES // width
    quad = row_count * fold // chan_local
    eight = row_count // quad
    span = 2 * SEG
    from_time = lax.broadcasted_iota(jnp.int32, (block_len, block_len), 0)
    to_time = lax.broadcasted_iota(jnp.int32, (block_len, block_len), 1)
    from_seg = lax.rem(from_time + block_len - LEAD, block_len) // SEG
    to_seg = lax.rem(to_time + block_len - LEAD, block_len) // SEG
    own_mask = (from_seg == to_seg) | (from_seg + 1 == to_seg)
    cross_mask = to_seg[:spectra] == 0
    no_rows = jnp.zeros((block_len - spectra, block_len), jnp.float32)
    lane = lax.broadcasted_iota(jnp.int32, (source_count * quad, block_len), 1) // spectra
    total[...] = jnp.zeros_like(total)

    def gathered(ref, number):
        return jnp.concatenate(
            [
                ref[pl.ds(q * eight + number, source_count, stride=PITCH), :]
                for q in range(quad)
            ],
            axis=0,
        )

    def turned(value, shift):
        return pltpu.roll(value, shift % LANES, 1) if shift % LANES else value

    def matrix(real, imag):
        return jnp.concatenate(
            [jnp.concatenate([real, imag], axis=1), jnp.concatenate([-imag, real], axis=1)], axis=0
        ).astype(jnp.bfloat16)

    for piece in range(piece_count):
        for source in range(source_count):
            held[piece, source * PITCH : source * PITCH + row_count] = spectra_ref[
                source, piece
            ].astype(jnp.float32)
    for source in range(source_count):
        held_tail[source * PITCH : source * PITCH + row_count] = tail_ref[source].astype(
            jnp.float32
        )

    def one(step, carry):
        for inner in range(UNROLL):
            number = step * UNROLL + inner
            pieces = [gathered(held.at[piece], number) for piece in range(piece_count)]
            tail = gathered(held_tail, number)
            for turn in range(fold):
                chan = number * fold + turn
                parts = []
                for pol in range(pol_count):
                    low = turn * width + pol * spectra
                    whole = turned(pieces[0], -low)
                    for piece in range(1, piece_count):
                        moved = turned(pieces[piece], piece * spectra - low)
                        whole = jnp.where(lane == piece, moved, whole)
                    parts.append(whole.astype(jnp.bfloat16))
                for pol in range(pol_count):
                    parts.append(
                        turned(tail, -(turn * width + pol * spectra)).astype(jnp.bfloat16)
                    )
                beams = jnp.dot(
                    weights_ref[chan],
                    jnp.concatenate(parts, axis=1),
                    preferred_element_type=jnp.float32,
                ).astype(jnp.bfloat16)

                def series(first):
                    return jnp.concatenate(
                        [
                            jnp.concatenate(
                                [
                                    beams[
                                        part * beam_count : (part + 1) * beam_count,
                                        (first + pol) * LANES : (first + pol + 1) * LANES,
                                    ]
                                    for part in range(2)
                                ],
                                axis=1,
                            )
                            for pol in range(pol_count)
                        ],
                        axis=0,
                    )

                kern = [kern_ref[chan, part] for part in range(2)]
                own = [
                    jnp.where(own_mask, jnp.concatenate([part] * (block_len // span), axis=0), 0.0)
                    for part in kern
                ]
                cross = [
                    jnp.concatenate(
                        [
                            jnp.where(
                                cross_mask,
                                jnp.concatenate([part[:LEAD], part[span - LEAD :]], axis=0),
                                0.0,
                            ),
                            no_rows,
                        ],
                        axis=0,
                    )
                    for part in kern
                ]
                clean = jnp.dot(
                    series(0), matrix(*own), preferred_element_type=jnp.float32
                ) + jnp.dot(
                    series(pol_count), matrix(*cross), preferred_element_type=jnp.float32
                )
                square = clean * clean
                both = square[:beam_count] + square[beam_count:]
                total[...] += both[:, :block_len] + both[:, block_len:]
        return carry

    lax.fori_loop(0, eight // UNROLL, one, 0)
    power_ref[...] = jnp.dot(
        total[...],
        order_ref[...],
        precision=lax.Precision.HIGHEST,
        preferred_element_type=jnp.float32,
    )


def shards(voltages, prototype, beam_delays, station_shifts, dm_index, owners):
    wide_count = lax.axis_size("wide")
    narrow_count = lax.axis_size("narrow")
    wide_index = lax.axis_index("wide")
    narrow_index = lax.axis_index("narrow")
    _, sub_count, station_local, pol_count, _, piece_len = voltages.shape
    tap_count, chan_count = prototype.shape
    beam_count, station_count = beam_delays.shape
    rows = station_local * pol_count * 2
    quad = station_local * 2
    spectra = piece_len // chan_count
    block_len = spectra * narrow_count
    chan_local = chan_count // narrow_count
    fold = LANES // (pol_count * spectra)
    fours = chan_count // fold
    members = min(2 * fold, sub_count // SHARES)
    whole = pl.BlockSpec(memory_space=pltpu.VMEM)
    scalars = pl.BlockSpec(memory_space=pltpu.SMEM)
    params = pltpu.CompilerParams(vmem_limit_bytes=VMEM_BYTES)

    volts = voltages.reshape(sub_count, rows, piece_len)

    def cut(first, last, low, high):
        return voltages[0, first:last, :, :, :, low:high].reshape(last - first, rows, high - low)

    ahead = (tap_count - 1 - LEAD) * chan_count + MAXD
    share = sub_count // SHARES
    ends = [
        (
            lax.ppermute(
                cut(i * share, (i + 1) * share, piece_len - LEAD * chan_count, piece_len),
                "narrow",
                [(i, (i + 1) % narrow_count) for i in range(narrow_count)],
            ),
            lax.ppermute(
                cut(i * share, (i + 1) * share, 0, ahead),
                "narrow",
                [(i, i - 1) for i in range(1, narrow_count)],
            ),
        )
        for i in range(SHARES)
    ]

    filler = -(tap_count + 1) % 8
    both = jnp.stack(
        [jnp.pad(prototype, ((0, filler + 1), (0, 0))), jnp.pad(prototype, ((1, filler), (0, 0)))]
    )
    ids = jnp.arange(chan_count, dtype=jnp.int32)
    row_chan = (ids % fours) * fold + ids // fours
    turn = jnp.mod(
        row_chan[None, :, None] * (ids[None, None, :] - station_shifts[:, None, None]), chan_count
    )
    angle = turn.astype(jnp.float32) * (TWO_PI / chan_count)
    scale = 1.0 / math.sqrt(chan_count)
    cosine, sine = jnp.cos(angle) * scale, jnp.sin(angle) * scale
    table = jnp.concatenate(
        [
            jnp.concatenate([cosine, sine], axis=2),
            jnp.concatenate([-sine, cosine], axis=2),
        ],
        axis=1,
    ).astype(jnp.bfloat16)
    packed = None
    for i, (left, right) in enumerate(ends):
        steps = share // members

        def block(length, first):
            return pl.BlockSpec((members, rows, length), lambda step: (step + first, 0, 0))

        packed = pl.pallas_call(
            filter_kernel,
            grid=(steps,),
            out_shape=jax.ShapeDtypeStruct((sub_count, fours * quad, LANES), jnp.bfloat16),
            in_specs=[
                scalars,
                scalars,
                block(piece_len, i * steps),
                block(LEAD * chan_count, 0),
                block(ahead, 0),
                whole,
                whole,
            ]
            + [pl.BlockSpec(memory_space=pl.ANY)] * min(i, 1),
            out_specs=pl.BlockSpec(
                (members, fours * quad, LANES), lambda step, first=i * steps: (step + first, 0, 0)
            ),
            scratch_shapes=[
                pltpu.VMEM((tap_count + 1, rows, chan_count), jnp.float32),
                pltpu.VMEM((chan_count // LANES, members * spectra * rows, LANES), jnp.float32),
                pltpu.VMEM((members, fours // 8, quad, 8, LANES), jnp.float32),
            ],
            input_output_aliases={7: 0} if i else {},
            compiler_params=pltpu.CompilerParams(vmem_limit_bytes=FILTER_VMEM),
            name="filter",
        )(
            narrow_index.astype(jnp.int32)[None],
            station_shifts,
            volts,
            left,
            right,
            both,
            table,
            *([packed] if i else []),
        )

    local_rows = fours * quad // narrow_count
    packed = packed.reshape(sub_count * narrow_count, local_rows, LANES)
    packed = lax.all_to_all(packed, ("wide", "narrow"), 0, 0, tiled=True)
    packed = packed.reshape(wide_count, narrow_count, local_rows, LANES)

    early = jnp.arange(LANES) % spectra < LEAD
    tail = jnp.where(early, packed[:, 0], packed[:, narrow_count - 1])
    tail = lax.ppermute(tail, "sec", [(0, 1)])

    sub = wide_index
    channels = narrow_index * chan_local + jnp.arange(chan_local, dtype=jnp.int32)
    frequency = sub.astype(jnp.float32) + channels.astype(jnp.float32) / chan_count
    delays = jnp.transpose(beam_delays.reshape(beam_count, wide_count, station_local), (0, 2, 1))
    delays = jnp.repeat(delays, 2, axis=1).reshape(beam_count, 2 * station_count)
    phase = (TWO_PI * frequency)[:, None, None] * delays[None]
    norm = 1.0 / math.sqrt(station_count)
    cosine, sine = jnp.cos(phase) * norm, jnp.sin(phase) * norm
    is_real = jnp.arange(2 * station_count)[None, None, :] // wide_count % 2 == 0
    weights = jnp.concatenate(
        [jnp.where(is_real, cosine, sine), jnp.where(is_real, -sine, cosine)], axis=1
    ).astype(jnp.bfloat16)

    span = 2 * SEG
    bins = jnp.arange(span, dtype=jnp.int32)
    signed = jnp.where(bins < span // 2, bins, bins - span)
    dm_value = jnp.sum(jnp.where(jnp.arange(sub_count) == sub, dm_index, 0))
    phase_index = dm_value * signed[None, :] * (signed[None, :] + channels[:, None])
    angle_index = jnp.mod(
        phase_index[:, None, :] + 2 * bins[None, :, None] * bins[None, None, :], 2 * span
    )
    angles = angle_index.astype(jnp.float32) * (math.pi / span)
    kern = jnp.stack(
        [jnp.sum(jnp.cos(angles), axis=-1) / span, jnp.sum(jnp.sin(angles), axis=-1) / span],
        axis=1,
    ).astype(jnp.bfloat16)
    times = jnp.arange(block_len, dtype=jnp.int32)
    lag = jnp.mod(times[None, :] - bins[:, None], span)
    pick = (lag[None] == bins[:, None, None]).astype(jnp.bfloat16)
    kern = jnp.einsum("crd,dab->crab", kern, pick, preferred_element_type=jnp.float32)
    order = (jnp.mod(times - LEAD, block_len)[:, None] == times[None, :]).astype(jnp.float32)

    partial = pl.pallas_call(
        beam_kernel,
        out_shape=jax.ShapeDtypeStruct((beam_count, block_len), jnp.float32),
        in_specs=[whole] * 5,
        out_specs=whole,
        scratch_shapes=[
            pltpu.VMEM((narrow_count, wide_count * PITCH, LANES), jnp.float32),
            pltpu.VMEM((wide_count * PITCH, LANES), jnp.float32),
            pltpu.VMEM((beam_count, block_len), jnp.float32),
        ],
        compiler_params=params,
        name="beams",
    )(packed, tail, weights, kern, order)

    partial = partial.reshape(narrow_count, beam_count // narrow_count, block_len)
    partial = lax.all_to_all(partial, "narrow", 0, 0, tiled=True)
    summed = jnp.sum(partial, axis=0) / chan_count
    subs = jnp.arange(sub_count, dtype=jnp.int32)
    owner = jnp.sum(jnp.where(subs == sub, owners, 0))
    goes = jnp.arange(wide_count, dtype=jnp.int32) == owner
    outgoing = jnp.where(goes[:, None, None], summed[None], 0.0)
    arrived = lax.all_to_all(outgoing, "wide", 0, 0, tiled=True)
    owned = owners == wide_index
    rank = jnp.cumsum(owned.astype(jnp.int32)) - 1
    slots = jnp.arange(SUBBAND_LIMIT, dtype=jnp.int32)
    held = owned[None, :] & (rank[None, :] == slots[:, None])
    chosen = jnp.sum(jnp.where(held, subs[None, :], 0), axis=1)
    result = jnp.take(arrived, chosen, axis=0)
    return jnp.where(jnp.any(held, axis=1)[:, None, None], result, 0.0)[None]


def solution(mesh):
    placed = (P("sec", None, "wide", None, None, "narrow"), P(), P(), P("wide"), P(), P())
    return jax.shard_map(
        shards,
        mesh=mesh,
        in_specs=placed,
        out_specs=P("sec", "wide", "narrow", None),
        check_vma=False,
    )
```

```python
import math

import jax
import jax.numpy as jnp
from jax import lax
from jax.experimental import pallas as pl
from jax.experimental.pallas import tpu as pltpu
from jax.sharding import PartitionSpec as P

SEG = 16
SUBBAND_LIMIT = 2
MAXD = 128
LEAD = 8
LANES = 128
TWO_PI = 2.0 * math.pi
UNROLL = 4
PITCH = 40
SHARES = 2
FILTER_VMEM = 63 * 1024 * 1024
VMEM_BYTES = 48 * 1024 * 1024


def filter_kernel(
    where_ref, shifts_ref, own_ref, left_ref, right_ref, prototype_ref, table_ref, *refs
):
    out_ref, taps_ref, filtered, packed = refs[-4:]
    members, rows, piece_len = own_ref.shape
    tap_count, _, chan_count = taps_ref.shape
    station_count = table_ref.shape[0]
    pol_count = rows // (2 * station_count)
    quad = 2 * station_count
    spectra = piece_len // chan_count
    halves = chan_count // LANES
    width = pol_count * spectra
    fold = LANES // width
    fours = chan_count // fold
    zero = jnp.zeros((rows, LANES), jnp.float32)

    @pl.when(pl.program_id(0) == 0)
    def _():
        lane = lax.broadcasted_iota(jnp.int32, prototype_ref.shape[1:], 1)
        moved = [
            jnp.where(
                lane < shifts_ref[station],
                pltpu.roll(prototype_ref[1], shifts_ref[station], 1),
                pltpu.roll(prototype_ref[0], shifts_ref[station], 1),
            )
            for station in range(station_count)
        ]
        row = lax.broadcasted_iota(jnp.int32, (rows, chan_count), 0) // (2 * pol_count)
        for tap in range(tap_count):
            whole = jnp.broadcast_to(moved[0][tap : tap + 1], (rows, chan_count))
            for station in range(1, station_count):
                other = jnp.broadcast_to(moved[station][tap : tap + 1], (rows, chan_count))
                whole = jnp.where(row == station, other, whole)
            taps_ref[tap] = whole

    follows = jnp.where(where_ref[0] == 0, 0.0, 1.0)

    def one_sub(member, inner):
        for half in range(halves):
            lanes = slice(half * LANES, half * LANES + LANES)
            taps = [taps_ref[tap, :, lanes] for tap in range(tap_count)]

            def load(ref, frame):
                low = frame * chan_count + half * LANES
                if low >= ref.shape[-1]:
                    return zero
                return ref[member, :, low : low + LANES].astype(jnp.float32)

            own = [load(own_ref, frame) for frame in range(spectra)]
            early = [load(left_ref, frame) for frame in range(LEAD)]
            early += [frame * follows for frame in own]
            late = own + [load(right_ref, frame) for frame in range(LEAD)]
            for number in range(spectra):
                source = early[number:] if number < LEAD else late[number - LEAD :]
                total = taps[0] * source[0]
                for tap in range(1, tap_count):
                    total = total + taps[tap] * source[tap]
                at = pl.multiple_of((member * spectra + number) * rows, rows)
                filtered[half, pl.ds(at, rows), :] = total
        return inner

    lax.fori_loop(0, members, one_sub, 0)
    lane = lax.broadcasted_iota(jnp.int32, (fours, LANES), 1) // width
    for station in range(station_count):
        parts = []
        for member in range(members):
            for pol in range(pol_count):
                first = member * spectra * rows + (station * pol_count + pol) * 2
                parts.append(
                    jnp.concatenate(
                        [
                            filtered[half, pl.ds(first + r, spectra, stride=rows), :].astype(
                                jnp.bfloat16
                            )
                            for r in range(2)
                            for half in range(halves)
                        ],
                        axis=1,
                    )
                )
        spectrum = lax.dot_general(
            table_ref[station],
            jnp.concatenate(parts, axis=0),
            (((1,), (1,)), ((), ())),
            preferred_element_type=jnp.float32,
        )
        for r in range(2):
            for tile in range(members // fold):
                blocks = [
                    spectrum[
                        (r * fold + turn) * fours : (r * fold + turn + 1) * fours,
                        tile * LANES : (tile + 1) * LANES,
                    ]
                    for turn in range(fold)
                ]
                step = fold // 2
                while step:
                    low = (lane // step) % 2 == 0
                    swapped = list(blocks)
                    for first in range(fold):
                        if first // step % 2 == 0:
                            a, b = blocks[first], blocks[first + step]
                            swapped[first] = jnp.where(low, a, pltpu.roll(b, step * width, 1))
                            swapped[first + step] = jnp.where(
                                low, pltpu.roll(a, LANES - step * width, 1), b
                            )
                    blocks = swapped
                    step //= 2
                for member, block in enumerate(blocks):
                    packed[tile * fold + member, :, station * 2 + r] = block.reshape(
                        fours // 8, 8, LANES
                    )
    for member in range(members):
        out_ref[:, member] = (
            packed[member].reshape(out_ref.shape[0], -1, LANES).astype(jnp.bfloat16)
        )


def beam_kernel(
    spectra_ref, tail_ref, weights_ref, kern_ref, order_ref, power_ref, held, held_tail, total
):
    piece_count, source_count, row_count, _ = spectra_ref.shape
    beam_count, block_len = power_ref.shape
    chan_local = weights_ref.shape[0]
    pol_count = 2
    spectra = block_len // piece_count
    width = pol_count * spectra
    fold = LANES // width
    quad = row_count * fold // chan_local
    eight = row_count // quad
    span = 2 * SEG
    from_time = lax.broadcasted_iota(jnp.int32, (block_len, block_len), 0)
    to_time = lax.broadcasted_iota(jnp.int32, (block_len, block_len), 1)
    from_seg = lax.rem(from_time + block_len - LEAD, block_len) // SEG
    to_seg = lax.rem(to_time + block_len - LEAD, block_len) // SEG
    own_mask = (from_seg == to_seg) | (from_seg + 1 == to_seg)
    cross_mask = to_seg[:spectra] == 0
    no_rows = jnp.zeros((block_len - spectra, block_len), jnp.float32)
    lane = lax.broadcasted_iota(jnp.int32, (source_count * quad, block_len), 1) // spectra
    total[...] = jnp.zeros_like(total)

    def gathered(ref, number):
        return jnp.concatenate(
            [
                ref[pl.ds(q * eight + number, source_count, stride=PITCH), :]
                for q in range(quad)
            ],
            axis=0,
        )

    def turned(value, shift):
        return pltpu.roll(value, shift % LANES, 1) if shift % LANES else value

    def matrix(real, imag):
        return jnp.concatenate(
            [jnp.concatenate([real, imag], axis=1), jnp.concatenate([-imag, real], axis=1)], axis=0
        ).astype(jnp.bfloat16)

    for piece in range(piece_count):
        for source in range(source_count):
            held[piece, source * PITCH : source * PITCH + row_count] = spectra_ref[
                piece, source
            ].astype(jnp.float32)
    for source in range(source_count):
        held_tail[source * PITCH : source * PITCH + row_count] = tail_ref[source].astype(
            jnp.float32
        )

    def one(step, carry):
        for inner in range(UNROLL):
            number = step * UNROLL + inner
            pieces = [gathered(held.at[piece], number) for piece in range(piece_count)]
            tail = gathered(held_tail, number)
            for turn in range(fold):
                chan = number * fold + turn
                parts = []
                for pol in range(pol_count):
                    low = turn * width + pol * spectra
                    whole = turned(pieces[0], -low)
                    for piece in range(1, piece_count):
                        moved = turned(pieces[piece], piece * spectra - low)
                        whole = jnp.where(lane == piece, moved, whole)
                    parts.append(whole.astype(jnp.bfloat16))
                for pol in range(pol_count):
                    parts.append(
                        turned(tail, -(turn * width + pol * spectra)).astype(jnp.bfloat16)
                    )
                beams = jnp.dot(
                    weights_ref[chan],
                    jnp.concatenate(parts, axis=1),
                    preferred_element_type=jnp.float32,
                ).astype(jnp.bfloat16)

                def series(first):
                    return jnp.concatenate(
                        [
                            jnp.concatenate(
                                [
                                    beams[
                                        part * beam_count : (part + 1) * beam_count,
                                        (first + pol) * LANES : (first + pol + 1) * LANES,
                                    ]
                                    for part in range(2)
                                ],
                                axis=1,
                            )
                            for pol in range(pol_count)
                        ],
                        axis=0,
                    )

                kern = [kern_ref[chan, part] for part in range(2)]
                own = [
                    jnp.where(own_mask, jnp.concatenate([part] * (block_len // span), axis=0), 0.0)
                    for part in kern
                ]
                cross = [
                    jnp.concatenate(
                        [
                            jnp.where(
                                cross_mask,
                                jnp.concatenate([part[:LEAD], part[span - LEAD :]], axis=0),
                                0.0,
                            ),
                            no_rows,
                        ],
                        axis=0,
                    )
                    for part in kern
                ]
                clean = jnp.dot(
                    series(0), matrix(*own), preferred_element_type=jnp.float32
                ) + jnp.dot(
                    series(pol_count), matrix(*cross), preferred_element_type=jnp.float32
                )
                square = clean * clean
                both = square[:beam_count] + square[beam_count:]
                total[...] += both[:, :block_len] + both[:, block_len:]
        return carry

    lax.fori_loop(0, eight // UNROLL, one, 0)
    power_ref[...] = jnp.dot(
        total[...],
        order_ref[...],
        precision=lax.Precision.HIGHEST,
        preferred_element_type=jnp.float32,
    )


def shards(voltages, prototype, beam_delays, station_shifts, dm_index, owners):
    wide_count = lax.axis_size("wide")
    narrow_count = lax.axis_size("narrow")
    wide_index = lax.axis_index("wide")
    narrow_index = lax.axis_index("narrow")
    _, sub_count, station_local, pol_count, _, piece_len = voltages.shape
    tap_count, chan_count = prototype.shape
    beam_count, station_count = beam_delays.shape
    rows = station_local * pol_count * 2
    quad = station_local * 2
    spectra = piece_len // chan_count
    block_len = spectra * narrow_count
    chan_local = chan_count // narrow_count
    fold = LANES // (pol_count * spectra)
    fours = chan_count // fold
    members = min(2 * fold, sub_count // SHARES)
    whole = pl.BlockSpec(memory_space=pltpu.VMEM)
    scalars = pl.BlockSpec(memory_space=pltpu.SMEM)
    params = pltpu.CompilerParams(vmem_limit_bytes=VMEM_BYTES)

    volts = voltages.reshape(sub_count, rows, piece_len)
    ahead = (tap_count - 1 - LEAD) * chan_count + MAXD
    share = sub_count // SHARES
    ends = [
        (
            lax.ppermute(
                volts[i * share : (i + 1) * share, :, piece_len - LEAD * chan_count :],
                "narrow",
                [(i, (i + 1) % narrow_count) for i in range(narrow_count)],
            ),
            lax.ppermute(
                volts[i * share : (i + 1) * share, :, :ahead],
                "narrow",
                [(i, i - 1) for i in range(1, narrow_count)],
            ),
        )
        for i in range(SHARES)
    ]

    filler = -(tap_count + 1) % 8
    both = jnp.stack(
        [jnp.pad(prototype, ((0, filler + 1), (0, 0))), jnp.pad(prototype, ((1, filler), (0, 0)))]
    )
    ids = jnp.arange(chan_count, dtype=jnp.int32)
    row_chan = (ids % fours) * fold + ids // fours
    turn = jnp.mod(
        row_chan[None, :, None] * (ids[None, None, :] - station_shifts[:, None, None]), chan_count
    )
    angle = turn.astype(jnp.float32) * (TWO_PI / chan_count)
    scale = 1.0 / math.sqrt(chan_count)
    cosine, sine = jnp.cos(angle) * scale, jnp.sin(angle) * scale
    table = jnp.concatenate(
        [
            jnp.concatenate([cosine, sine], axis=2),
            jnp.concatenate([-sine, cosine], axis=2),
        ],
        axis=1,
    ).astype(jnp.bfloat16)
    local_rows = fours * quad // narrow_count
    packed = None
    for i, (left, right) in enumerate(ends):
        steps = share // members

        def block(length, first):
            return pl.BlockSpec((members, rows, length), lambda step: (step + first, 0, 0))

        packed = pl.pallas_call(
            filter_kernel,
            grid=(steps,),
            out_shape=jax.ShapeDtypeStruct(
                (narrow_count, sub_count, local_rows, LANES), jnp.bfloat16
            ),
            in_specs=[
                scalars,
                scalars,
                block(piece_len, i * steps),
                block(LEAD * chan_count, 0),
                block(ahead, 0),
                whole,
                whole,
            ]
            + [pl.BlockSpec(memory_space=pl.ANY)] * min(i, 1),
            out_specs=pl.BlockSpec(
                (narrow_count, members, local_rows, LANES),
                lambda step, first=i * steps: (0, step + first, 0, 0),
            ),
            scratch_shapes=[
                pltpu.VMEM((tap_count + 1, rows, chan_count), jnp.float32),
                pltpu.VMEM((chan_count // LANES, members * spectra * rows, LANES), jnp.float32),
                pltpu.VMEM((members, fours // 8, quad, 8, LANES), jnp.float32),
            ],
            input_output_aliases={7: 0} if i else {},
            compiler_params=pltpu.CompilerParams(vmem_limit_bytes=FILTER_VMEM),
            name="filter",
        )(
            narrow_index.astype(jnp.int32)[None],
            station_shifts,
            volts,
            left,
            right,
            both,
            table,
            *([packed] if i else []),
        )

    packed = packed.reshape(sub_count * narrow_count, local_rows, LANES)
    packed = lax.all_to_all(packed, ("narrow", "wide"), 0, 0, tiled=True)
    packed = packed.reshape(narrow_count, wide_count, local_rows, LANES)

    early = jnp.arange(LANES) % spectra < LEAD
    tail = jnp.where(early, packed[0], packed[narrow_count - 1])
    tail = lax.ppermute(tail, "sec", [(0, 1)])

    sub = wide_index
    channels = narrow_index * chan_local + jnp.arange(chan_local, dtype=jnp.int32)
    frequency = sub.astype(jnp.float32) + channels.astype(jnp.float32) / chan_count
    delays = jnp.transpose(beam_delays.reshape(beam_count, wide_count, station_local), (0, 2, 1))
    delays = jnp.repeat(delays, 2, axis=1).reshape(beam_count, 2 * station_count)
    phase = (TWO_PI * frequency)[:, None, None] * delays[None]
    norm = 1.0 / math.sqrt(station_count)
    cosine, sine = jnp.cos(phase) * norm, jnp.sin(phase) * norm
    is_real = jnp.arange(2 * station_count)[None, None, :] // wide_count % 2 == 0
    weights = jnp.concatenate(
        [jnp.where(is_real, cosine, sine), jnp.where(is_real, -sine, cosine)], axis=1
    ).astype(jnp.bfloat16)

    span = 2 * SEG
    bins = jnp.arange(span, dtype=jnp.int32)
    signed = jnp.where(bins < span // 2, bins, bins - span)
    dm_value = jnp.sum(jnp.where(jnp.arange(sub_count) == sub, dm_index, 0))
    phase_index = dm_value * signed[None, :] * (signed[None, :] + channels[:, None])
    angle_index = jnp.mod(
        phase_index[:, None, :] + 2 * bins[None, :, None] * bins[None, None, :], 2 * span
    )
    angles = angle_index.astype(jnp.float32) * (math.pi / span)
    kern = jnp.stack(
        [jnp.sum(jnp.cos(angles), axis=-1) / span, jnp.sum(jnp.sin(angles), axis=-1) / span],
        axis=1,
    ).astype(jnp.bfloat16)
    times = jnp.arange(block_len, dtype=jnp.int32)
    lag = jnp.mod(times[None, :] - bins[:, None], span)
    pick = (lag[None] == bins[:, None, None]).astype(jnp.bfloat16)
    kern = jnp.einsum("crd,dab->crab", kern, pick, preferred_element_type=jnp.float32)
    order = (jnp.mod(times - LEAD, block_len)[:, None] == times[None, :]).astype(jnp.float32)

    partial = pl.pallas_call(
        beam_kernel,
        out_shape=jax.ShapeDtypeStruct((beam_count, block_len), jnp.float32),
        in_specs=[whole] * 5,
        out_specs=whole,
        scratch_shapes=[
            pltpu.VMEM((narrow_count, wide_count * PITCH, LANES), jnp.float32),
            pltpu.VMEM((wide_count * PITCH, LANES), jnp.float32),
            pltpu.VMEM((beam_count, block_len), jnp.float32),
        ],
        compiler_params=params,
        name="beams",
    )(packed, tail, weights, kern, order)

    partial = partial.reshape(narrow_count, beam_count // narrow_count, block_len)
    partial = lax.all_to_all(partial, "narrow", 0, 0, tiled=True)
    summed = jnp.sum(partial, axis=0) / chan_count
    subs = jnp.arange(sub_count, dtype=jnp.int32)
    owner = jnp.sum(jnp.where(subs == sub, owners, 0))
    goes = jnp.arange(wide_count, dtype=jnp.int32) == owner
    outgoing = jnp.where(goes[:, None, None], summed[None], 0.0)
    arrived = lax.all_to_all(outgoing, "wide", 0, 0, tiled=True)
    owned = owners == wide_index
    rank = jnp.cumsum(owned.astype(jnp.int32)) - 1
    slots = jnp.arange(SUBBAND_LIMIT, dtype=jnp.int32)
    held = owned[None, :] & (rank[None, :] == slots[:, None])
    chosen = held[:, :, None, None]
    return jnp.sum(jnp.where(chosen, arrived[None], 0.0), axis=1)[None]


def solution(mesh):
    placed = (P("sec", None, "wide", None, None, "narrow"), P(), P(), P("wide"), P(), P())
    return jax.shard_map(
        shards,
        mesh=mesh,
        in_specs=placed,
        out_specs=P("sec", "wide", "narrow", None),
        check_vma=False,
    )
```

```python
import math

import jax
import jax.numpy as jnp
from jax import lax
from jax.experimental import pallas as pl
from jax.experimental.pallas import tpu as pltpu
from jax.sharding import PartitionSpec as P

SEG = 16
SUBBAND_LIMIT = 2
MAXD = 128
LEAD = 8
LANES = 128
TWO_PI = 2.0 * math.pi
UNROLL = 8
PITCH = 40
SHARES = 2
FILTER_VMEM = 63 * 1024 * 1024
VMEM_BYTES = 48 * 1024 * 1024


def filter_kernel(
    where_ref, shifts_ref, own_ref, left_ref, right_ref, prototype_ref, table_ref, *refs
):
    out_ref, taps_ref, filtered, packed = refs[-4:]
    members, rows, piece_len = own_ref.shape
    tap_count, _, chan_count = taps_ref.shape
    station_count = table_ref.shape[0]
    pol_count = rows // (2 * station_count)
    quad = 2 * station_count
    spectra = piece_len // chan_count
    halves = chan_count // LANES
    width = pol_count * spectra
    fold = LANES // width
    fours = chan_count // fold
    zero = jnp.zeros((rows, LANES), jnp.float32)

    @pl.when(pl.program_id(0) == 0)
    def _():
        lane = lax.broadcasted_iota(jnp.int32, prototype_ref.shape[1:], 1)
        moved = [
            jnp.where(
                lane < shifts_ref[station],
                pltpu.roll(prototype_ref[1], shifts_ref[station], 1),
                pltpu.roll(prototype_ref[0], shifts_ref[station], 1),
            )
            for station in range(station_count)
        ]
        row = lax.broadcasted_iota(jnp.int32, (rows, chan_count), 0) // (2 * pol_count)
        for tap in range(tap_count):
            whole = jnp.broadcast_to(moved[0][tap : tap + 1], (rows, chan_count))
            for station in range(1, station_count):
                other = jnp.broadcast_to(moved[station][tap : tap + 1], (rows, chan_count))
                whole = jnp.where(row == station, other, whole)
            taps_ref[tap] = whole

    follows = jnp.where(where_ref[0] == 0, 0.0, 1.0)

    def one_sub(member, inner):
        for half in range(halves):
            lanes = slice(half * LANES, half * LANES + LANES)
            taps = [taps_ref[tap, :, lanes] for tap in range(tap_count)]

            def load(ref, frame):
                low = frame * chan_count + half * LANES
                if low >= ref.shape[-1]:
                    return zero
                return ref[member, :, low : low + LANES].astype(jnp.float32)

            own = [load(own_ref, frame) for frame in range(spectra)]
            early = [load(left_ref, frame) for frame in range(LEAD)]
            early += [frame * follows for frame in own]
            late = own + [load(right_ref, frame) for frame in range(LEAD)]
            for number in range(spectra):
                source = early[number:] if number < LEAD else late[number - LEAD :]
                total = taps[0] * source[0]
                for tap in range(1, tap_count):
                    total = total + taps[tap] * source[tap]
                at = pl.multiple_of((member * spectra + number) * rows, rows)
                filtered[half, pl.ds(at, rows), :] = total
        return inner

    lax.fori_loop(0, members, one_sub, 0, unroll=2)
    lane = lax.broadcasted_iota(jnp.int32, (fours, LANES), 1) // width
    for station in range(station_count):
        parts = []
        for member in range(members):
            for pol in range(pol_count):
                first = member * spectra * rows + (station * pol_count + pol) * 2
                parts.append(
                    jnp.concatenate(
                        [
                            filtered[half, pl.ds(first + r, spectra, stride=rows), :].astype(
                                jnp.bfloat16
                            )
                            for r in range(2)
                            for half in range(halves)
                        ],
                        axis=1,
                    )
                )
        spectrum = lax.dot_general(
            table_ref[station],
            jnp.concatenate(parts, axis=0),
            (((1,), (1,)), ((), ())),
            preferred_element_type=jnp.float32,
        )
        for r in range(2):
            for tile in range(members // fold):
                blocks = [
                    spectrum[
                        (r * fold + turn) * fours : (r * fold + turn + 1) * fours,
                        tile * LANES : (tile + 1) * LANES,
                    ]
                    for turn in range(fold)
                ]
                step = fold // 2
                while step:
                    low = (lane // step) % 2 == 0
                    swapped = list(blocks)
                    for first in range(fold):
                        if first // step % 2 == 0:
                            a, b = blocks[first], blocks[first + step]
                            swapped[first] = jnp.where(low, a, pltpu.roll(b, step * width, 1))
                            swapped[first + step] = jnp.where(
                                low, pltpu.roll(a, LANES - step * width, 1), b
                            )
                    blocks = swapped
                    step //= 2
                for member, block in enumerate(blocks):
                    packed[tile * fold + member, :, station * 2 + r] = block.reshape(
                        fours // 8, 8, LANES
                    )
    for member in range(members):
        out_ref[:, member] = (
            packed[member].reshape(out_ref.shape[0], -1, LANES).astype(jnp.bfloat16)
        )


def beam_kernel(
    spectra_ref, tail_ref, weights_ref, kern_ref, order_ref, power_ref, held, held_tail, total
):
    piece_count, source_count, row_count, _ = spectra_ref.shape
    beam_count, block_len = power_ref.shape
    chan_local = weights_ref.shape[0]
    pol_count = 2
    spectra = block_len // piece_count
    width = pol_count * spectra
    fold = LANES // width
    quad = row_count * fold // chan_local
    eight = row_count // quad
    span = 2 * SEG
    from_time = lax.broadcasted_iota(jnp.int32, (block_len, block_len), 0)
    to_time = lax.broadcasted_iota(jnp.int32, (block_len, block_len), 1)
    from_seg = lax.rem(from_time + block_len - LEAD, block_len) // SEG
    to_seg = lax.rem(to_time + block_len - LEAD, block_len) // SEG
    own_mask = (from_seg == to_seg) | (from_seg + 1 == to_seg)
    cross_mask = to_seg[:spectra] == 0
    no_rows = jnp.zeros((block_len - spectra, block_len), jnp.float32)
    lane = lax.broadcasted_iota(jnp.int32, (source_count * quad, block_len), 1) // spectra
    total[...] = jnp.zeros_like(total)

    def gathered(ref, number):
        return jnp.concatenate(
            [
                ref[pl.ds(q * eight + number, source_count, stride=PITCH), :]
                for q in range(quad)
            ],
            axis=0,
        )

    def turned(value, shift):
        return pltpu.roll(value, shift % LANES, 1) if shift % LANES else value

    def matrix(real, imag):
        return jnp.concatenate(
            [jnp.concatenate([real, imag], axis=1), jnp.concatenate([-imag, real], axis=1)], axis=0
        ).astype(jnp.bfloat16)

    for piece in range(piece_count):
        for source in range(source_count):
            held[piece, source * PITCH : source * PITCH + row_count] = spectra_ref[
                piece, source
            ].astype(jnp.float32)
    for source in range(source_count):
        held_tail[source * PITCH : source * PITCH + row_count] = tail_ref[source].astype(
            jnp.float32
        )

    def one(step, carry):
        for inner in range(UNROLL):
            number = step * UNROLL + inner
            pieces = [gathered(held.at[piece], number) for piece in range(piece_count)]
            tail = gathered(held_tail, number)
            for turn in range(fold):
                chan = number * fold + turn
                parts = []
                for pol in range(pol_count):
                    low = turn * width + pol * spectra
                    whole = turned(pieces[0], -low)
                    for piece in range(1, piece_count):
                        moved = turned(pieces[piece], piece * spectra - low)
                        whole = jnp.where(lane == piece, moved, whole)
                    parts.append(whole.astype(jnp.bfloat16))
                for pol in range(pol_count):
                    parts.append(
                        turned(tail, -(turn * width + pol * spectra)).astype(jnp.bfloat16)
                    )
                beams = jnp.dot(
                    weights_ref[chan],
                    jnp.concatenate(parts, axis=1),
                    preferred_element_type=jnp.float32,
                ).astype(jnp.bfloat16)

                def series(first):
                    return jnp.concatenate(
                        [
                            jnp.concatenate(
                                [
                                    beams[
                                        part * beam_count : (part + 1) * beam_count,
                                        (first + pol) * LANES : (first + pol + 1) * LANES,
                                    ]
                                    for part in range(2)
                                ],
                                axis=1,
                            )
                            for pol in range(pol_count)
                        ],
                        axis=0,
                    )

                kern = [kern_ref[chan, part] for part in range(2)]
                own = [
                    jnp.where(own_mask, jnp.concatenate([part] * (block_len // span), axis=0), 0.0)
                    for part in kern
                ]
                cross = [
                    jnp.concatenate(
                        [
                            jnp.where(
                                cross_mask,
                                jnp.concatenate([part[:LEAD], part[span - LEAD :]], axis=0),
                                0.0,
                            ),
                            no_rows,
                        ],
                        axis=0,
                    )
                    for part in kern
                ]
                clean = jnp.dot(
                    series(0), matrix(*own), preferred_element_type=jnp.float32
                ) + jnp.dot(
                    series(pol_count), matrix(*cross), preferred_element_type=jnp.float32
                )
                square = clean * clean
                both = square[:beam_count] + square[beam_count:]
                total[...] += both[:, :block_len] + both[:, block_len:]
        return carry

    lax.fori_loop(0, eight // UNROLL, one, 0)
    power_ref[...] = jnp.dot(
        total[...],
        order_ref[...],
        precision=lax.Precision.HIGHEST,
        preferred_element_type=jnp.float32,
    )


def shards(voltages, prototype, beam_delays, station_shifts, dm_index, owners):
    wide_count = lax.axis_size("wide")
    narrow_count = lax.axis_size("narrow")
    wide_index = lax.axis_index("wide")
    narrow_index = lax.axis_index("narrow")
    _, sub_count, station_local, pol_count, _, piece_len = voltages.shape
    tap_count, chan_count = prototype.shape
    beam_count, station_count = beam_delays.shape
    rows = station_local * pol_count * 2
    quad = station_local * 2
    spectra = piece_len // chan_count
    block_len = spectra * narrow_count
    chan_local = chan_count // narrow_count
    fold = LANES // (pol_count * spectra)
    fours = chan_count // fold
    members = min(2 * fold, sub_count // SHARES)
    whole = pl.BlockSpec(memory_space=pltpu.VMEM)
    scalars = pl.BlockSpec(memory_space=pltpu.SMEM)
    params = pltpu.CompilerParams(vmem_limit_bytes=VMEM_BYTES)

    volts = voltages.reshape(sub_count, rows, piece_len)
    ahead = (tap_count - 1 - LEAD) * chan_count + MAXD
    share = sub_count // SHARES
    ends = [
        (
            lax.ppermute(
                volts[i * share : (i + 1) * share, :, piece_len - LEAD * chan_count :],
                "narrow",
                [(i, (i + 1) % narrow_count) for i in range(narrow_count)],
            ),
            lax.ppermute(
                volts[i * share : (i + 1) * share, :, :ahead],
                "narrow",
                [(i, i - 1) for i in range(1, narrow_count)],
            ),
        )
        for i in range(SHARES)
    ]

    filler = -(tap_count + 1) % 8
    both = jnp.stack(
        [jnp.pad(prototype, ((0, filler + 1), (0, 0))), jnp.pad(prototype, ((1, filler), (0, 0)))]
    )
    ids = jnp.arange(chan_count, dtype=jnp.int32)
    row_chan = (ids % fours) * fold + ids // fours
    turn = jnp.mod(
        row_chan[None, :, None] * (ids[None, None, :] - station_shifts[:, None, None]), chan_count
    )
    angle = turn.astype(jnp.float32) * (TWO_PI / chan_count)
    scale = 1.0 / math.sqrt(chan_count)
    cosine, sine = jnp.cos(angle) * scale, jnp.sin(angle) * scale
    table = jnp.concatenate(
        [
            jnp.concatenate([cosine, sine], axis=2),
            jnp.concatenate([-sine, cosine], axis=2),
        ],
        axis=1,
    ).astype(jnp.bfloat16)
    local_rows = fours * quad // narrow_count
    packed = None
    for i, (left, right) in enumerate(ends):
        steps = share // members

        def block(length, first):
            return pl.BlockSpec((members, rows, length), lambda step: (step + first, 0, 0))

        packed = pl.pallas_call(
            filter_kernel,
            grid=(steps,),
            out_shape=jax.ShapeDtypeStruct(
                (narrow_count, sub_count, local_rows, LANES), jnp.bfloat16
            ),
            in_specs=[
                scalars,
                scalars,
                block(piece_len, i * steps),
                block(LEAD * chan_count, 0),
                block(ahead, 0),
                whole,
                whole,
            ]
            + [pl.BlockSpec(memory_space=pl.ANY)] * min(i, 1),
            out_specs=pl.BlockSpec(
                (narrow_count, members, local_rows, LANES),
                lambda step, first=i * steps: (0, step + first, 0, 0),
            ),
            scratch_shapes=[
                pltpu.VMEM((tap_count + 1, rows, chan_count), jnp.float32),
                pltpu.VMEM((chan_count // LANES, members * spectra * rows, LANES), jnp.float32),
                pltpu.VMEM((members, fours // 8, quad, 8, LANES), jnp.float32),
            ],
            input_output_aliases={7: 0} if i else {},
            compiler_params=pltpu.CompilerParams(vmem_limit_bytes=FILTER_VMEM),
            name="filter",
        )(
            narrow_index.astype(jnp.int32)[None],
            station_shifts,
            volts,
            left,
            right,
            both,
            table,
            *([packed] if i else []),
        )

    packed = packed.reshape(sub_count * narrow_count, local_rows, LANES)
    packed = lax.all_to_all(packed, ("narrow", "wide"), 0, 0, tiled=True)
    packed = packed.reshape(narrow_count, wide_count, local_rows, LANES)

    early = jnp.arange(LANES) % spectra < LEAD
    tail = jnp.where(early, packed[0], packed[narrow_count - 1])
    tail = lax.ppermute(tail, "sec", [(0, 1)])

    sub = wide_index
    channels = narrow_index * chan_local + jnp.arange(chan_local, dtype=jnp.int32)
    frequency = sub.astype(jnp.float32) + channels.astype(jnp.float32) / chan_count
    delays = jnp.transpose(beam_delays.reshape(beam_count, wide_count, station_local), (0, 2, 1))
    delays = jnp.repeat(delays, 2, axis=1).reshape(beam_count, 2 * station_count)
    phase = (TWO_PI * frequency)[:, None, None] * delays[None]
    norm = 1.0 / math.sqrt(station_count)
    cosine, sine = jnp.cos(phase) * norm, jnp.sin(phase) * norm
    is_real = jnp.arange(2 * station_count)[None, None, :] // wide_count % 2 == 0
    weights = jnp.concatenate(
        [jnp.where(is_real, cosine, sine), jnp.where(is_real, -sine, cosine)], axis=1
    ).astype(jnp.bfloat16)

    span = 2 * SEG
    bins = jnp.arange(span, dtype=jnp.int32)
    signed = jnp.where(bins < span // 2, bins, bins - span)
    dm_value = jnp.sum(jnp.where(jnp.arange(sub_count) == sub, dm_index, 0))
    phase_index = dm_value * signed[None, :] * (signed[None, :] + channels[:, None])
    angle_index = jnp.mod(
        phase_index[:, None, :] + 2 * bins[None, :, None] * bins[None, None, :], 2 * span
    )
    angles = angle_index.astype(jnp.float32) * (math.pi / span)
    kern = jnp.stack(
        [jnp.sum(jnp.cos(angles), axis=-1) / span, jnp.sum(jnp.sin(angles), axis=-1) / span],
        axis=1,
    ).astype(jnp.bfloat16)
    times = jnp.arange(block_len, dtype=jnp.int32)
    lag = jnp.mod(times[None, :] - bins[:, None], span)
    pick = (lag[None] == bins[:, None, None]).astype(jnp.bfloat16)
    kern = jnp.einsum("crd,dab->crab", kern, pick, preferred_element_type=jnp.float32)
    order = (jnp.mod(times - LEAD, block_len)[:, None] == times[None, :]).astype(jnp.float32)

    partial = pl.pallas_call(
        beam_kernel,
        out_shape=jax.ShapeDtypeStruct((beam_count, block_len), jnp.float32),
        in_specs=[whole] * 5,
        out_specs=whole,
        scratch_shapes=[
            pltpu.VMEM((narrow_count, wide_count * PITCH, LANES), jnp.float32),
            pltpu.VMEM((wide_count * PITCH, LANES), jnp.float32),
            pltpu.VMEM((beam_count, block_len), jnp.float32),
        ],
        compiler_params=params,
        name="beams",
    )(packed, tail, weights, kern, order)

    partial = partial.reshape(narrow_count, beam_count // narrow_count, block_len)
    partial = lax.all_to_all(partial, "narrow", 0, 0, tiled=True)
    summed = jnp.sum(partial, axis=0) / chan_count
    subs = jnp.arange(sub_count, dtype=jnp.int32)
    owner = jnp.sum(jnp.where(subs == sub, owners, 0))
    goes = jnp.arange(wide_count, dtype=jnp.int32) == owner
    outgoing = jnp.where(goes[:, None, None], summed[None], 0.0)
    arrived = lax.all_to_all(outgoing, "wide", 0, 0, tiled=True)
    owned = owners == wide_index
    rank = jnp.cumsum(owned.astype(jnp.int32)) - 1
    slots = jnp.arange(SUBBAND_LIMIT, dtype=jnp.int32)
    held = owned[None, :] & (rank[None, :] == slots[:, None])
    chosen = held[:, :, None, None]
    return jnp.sum(jnp.where(chosen, arrived[None], 0.0), axis=1)[None]


def solution(mesh):
    placed = (P("sec", None, "wide", None, None, "narrow"), P(), P(), P("wide"), P(), P())
    return jax.shard_map(
        shards,
        mesh=mesh,
        in_specs=placed,
        out_specs=P("sec", "wide", "narrow", None),
        check_vma=False,
    )
```
